32 devices in a mesh: aux: 4 (over y, x), occ: 8 (over z, core).
Axes of the slice: x: 2, y: 2, z: 4, core: 2. Of those that a mesh axis runs over, the one named last changes fastest.
Arguments:
- integrals: bfloat16 [8, 192, 128, 128], P('aux', 'occ'), may hold values from -2 to 2
- coefficients: bfloat16 [4096, 384], P('occ'), may hold values from -0.3125 to 0.3125
- pair_rows: int32 [4, 192], P('aux', 'occ'), may hold values from 0 to 3
- pair_cols: int32 [4, 192], P('aux', 'occ'), may hold values from 0 to 31
- pair_count: int32 [4, 8], P('aux', 'occ'), may hold values from 1 to 24, as said below
- row_blocks: int32 [32], replicated, may hold values from 0 to 31, each once
Outputs:
- exchange_matrix: float32 [4096, 4096], P('aux', 'occ')
The draws below stay inside these ranges and needn't reach their ends.
Inputs may be any that keep to these rules, and one draw needn't show every extreme that they name: `pair_count`: at most 24 live slots for each auxiliary block and row owner, and some auxiliary block and owner has exactly 24.
All inputs are finite; a program needn't handle non-finite values.
Results may differ from the reference program's by a relative error of at most 0.0022.
Values may be sent and summed in bfloat16 or wider, within the bound.
No kernel may reach another device: no remote copies, remote signals or barrier semaphores. Data moves between devices by JAX's collectives and lax.ppermute only.
A program may use at most 64 MiB of HBM per device.

```python
import jax
import jax.numpy as jnp
from jax import lax

BS = 128
NBLK = 32
O = 384
PAIRS_DEV = 24
AUX_DEV = 2
NBAS = 4096
RB = 4
AUXBLK = 4
OCCBLK = 8
NAUX = 8


def draw_pair_count(key, part):
    first, second = jax.random.split(key)
    counts = jax.random.randint(first, (AUXBLK * OCCBLK,), 1, PAIRS_DEV + 1)
    chosen = jax.random.randint(second, (), 0, AUXBLK * OCCBLK)
    counts = jnp.where(jnp.arange(AUXBLK * OCCBLK) == chosen, PAIRS_DEV, counts)
    return counts.reshape(AUXBLK, OCCBLK).astype(jnp.int32)


def place_ends(drawn, rng, low, top_value):
    longest = drawn.shape.index(max(drawn.shape))
    spots = []
    for shift in (0, 1):
        where = [jax.random.randint(jax.random.fold_in(rng, axis), (), 0, length) for axis, length in enumerate(drawn.shape)]
        where[longest] = (where[longest] + shift) % drawn.shape[longest]
        spots.append(tuple(where))
    return drawn.at[spots[0]].set(low).at[spots[1]].set(top_value)


def steps_of(stream_key, shape, pieces, least, high):
    def one(dim, shards_of):
        heights = jax.random.uniform(jax.random.fold_in(jax.random.fold_in(stream_key, 6), dim), (shards_of,), jnp.float32, least / len(pieces), high / len(pieces))
        return jnp.repeat(jnp.exp(heights), shape[dim] // shards_of).reshape((-1,) + (1,) * (len(shape) - dim - 1))

    loudness = one(*pieces[0])
    for cut in pieces[1:]:
        loudness = loudness * one(*cut)
    return loudness


def centred(stream_key, dims, deviation, most, shards=(), held_as=jnp.bfloat16):
    values = jax.random.normal(stream_key, dims, jnp.float32) * deviation
    if len(shards) > 0:
        values = steps_of(stream_key, dims, shards, -0.22, 0.18) * values
    return jnp.clip(values, min=-most, max=most).astype(held_as)


def setup_inputs(seed: int = 0) -> dict:
    splits = jax.random.split(jax.random.key(seed), 7)
    return {
        "integrals": centred(splits[0], (NAUX, PAIRS_DEV * OCCBLK, BS, BS), ((NAUX * O) ** -0.25), 2.0, ((0, 4), (1, 8))),
        "coefficients": centred(splits[1], (NBAS, O), (BS * PAIRS_DEV // (2 * RB)) ** -0.5, 0.3125, ((0, 8),)),
        "pair_rows": place_ends(jax.random.randint(splits[2], (AUXBLK, PAIRS_DEV * OCCBLK), 0, RB), jax.random.fold_in(splits[2], 1), 0, RB - 1).astype(jnp.int32),
        "pair_cols": place_ends(jax.random.randint(splits[3], (AUXBLK, PAIRS_DEV * OCCBLK), 0, NBLK), jax.random.fold_in(splits[3], 1), 0, NBLK - 1).astype(jnp.int32),
        "pair_count": draw_pair_count(jax.random.fold_in(splits[6], 71), 0),
        "row_blocks": jax.random.permutation(splits[5], NBLK).astype(jnp.int32),
    }


def reference(integrals, coefficients, pair_rows, pair_cols, pair_count, row_blocks):
    coeff_blocks = coefficients.reshape(NBLK, BS, O).astype(jnp.float32)
    slot_index = jnp.arange(PAIRS_DEV * OCCBLK, dtype=jnp.int32)
    owner = slot_index // PAIRS_DEV
    position = slot_index % PAIRS_DEV
    block_ids = jnp.arange(NBLK, dtype=jnp.int32)
    integral_view = integrals.reshape(AUXBLK, AUX_DEV, PAIRS_DEV * OCCBLK, BS, BS)

    def one_block(total, inputs):
        block_ints, block_rows, block_cols, block_count = inputs
        live = position < block_count[owner]
        target = owner * RB + block_rows
        gathered = coeff_blocks[row_blocks[block_cols]]
        products = jnp.einsum("pkmn,kni->pkmi", block_ints.astype(jnp.float32), gathered)
        placing = ((target[:, None] == block_ids[None, :]) & live[:, None]).astype(jnp.float32)
        half = jnp.einsum("pkmi,kb->pbmi", products, placing).reshape(AUX_DEV, NBAS, O)
        half = lax.optimization_barrier(half.astype(jnp.bfloat16)).astype(jnp.float32)
        total = total + jnp.einsum("pni,pmi->nm", half, half)
        return total, None

    start = jnp.zeros((NBAS, NBAS), jnp.float32)
    total, unused = lax.scan(one_block, start, (integral_view, pair_rows, pair_cols, pair_count))
    return total
```

```python
import functools
import math

import jax
import jax.numpy as jnp
from jax import lax
from jax.experimental import pallas as pl
from jax.experimental.pallas import tpu as pltpu
from jax.sharding import PartitionSpec as P

AXES = ("aux", "occ")
CORES = 2
ANY = pl.BlockSpec(memory_space=pl.ANY)
IN_SMEM = pl.BlockSpec(memory_space=pltpu.SMEM)
IN_VMEM = pl.BlockSpec(memory_space=pltpu.VMEM)


class Layout:
    def __init__(self, aux, occ):
        self.aux, self.occ, self.planes = aux, occ, occ // CORES
        self.bits = int(math.log2(aux))

    def send(self, value, where):
        pairs = []
        for a in range(self.aux):
            for z in range(self.planes):
                for c in range(CORES):
                    to = where(a, z, c)
                    if to is not None:
                        pairs.append((a * self.occ + z * CORES + c, to[0] * self.occ + to[1] * CORES + to[2]))
        return lax.ppermute(value, AXES, pairs)


def half_kernel(lay, share, sources, count_ref, cols_ref, rows_ref, natural_ref, integrals_ref, *refs):
    pieces, (out_ref, coeff, total, sems) = refs[:sources], refs[sources:]
    own_blocks = total.shape[0]
    part = own_blocks // share
    copies = []
    start = 0
    for n, piece in enumerate(pieces):
        size = piece.shape[0]
        copies.append(pltpu.make_async_copy(piece, coeff.at[pl.ds(start, size)], sems.at[n]))
        start += size
    for copy in copies:
        copy.start()
    total[...] = jnp.zeros_like(total)
    for copy in copies:
        copy.wait()
    aux_count, slots, block, _ = integrals_ref.shape
    orbitals = coeff.shape[2]
    occ_index = lax.axis_index("occ")
    z, c = occ_index // CORES, occ_index % CORES
    k = lax.axis_index("aux") % share
    per_piece = (lay.planes - 1) * part

    def add_slot(slot, carry):
        natural = natural_ref[cols_ref[0, slot]]
        source, inner = natural // own_blocks, natural % own_blocks
        z_off, c_off = (source // CORES) ^ z, (source % CORES) ^ c
        k_off, in_part = (inner // part) ^ k, inner % part
        near = c_off * own_blocks + inner
        away = CORES * own_blocks + (k_off * CORES + c_off) * per_piece + (z_off - 1) * part + in_part
        piece = coeff[jnp.where(z_off == 0, near, away)]
        left = jnp.concatenate([integrals_ref[p, slot] for p in range(aux_count)], axis=0)
        total[rows_ref[0, slot]] += jnp.dot(left, piece, preferred_element_type=jnp.float32)
        return carry

    lax.fori_loop(0, count_ref[0, 0], add_slot, 0)
    for row in range(own_blocks):
        for p in range(aux_count):
            out_ref[pl.ds(row * block, block), pl.ds(p * orbitals, orbitals)] = total[
                row, pl.ds(p * block, block), :
            ].astype(jnp.bfloat16)


def half_transform(lay, share, own_blocks, integrals, pieces, cols, rows, count, natural):
    aux_count, slots, block, _ = integrals.shape
    orbitals = pieces[0].shape[2]
    blocks = sum(piece.shape[0] for piece in pieces)
    return pl.pallas_call(
        functools.partial(half_kernel, lay, share, len(pieces)),
        out_shape=jax.ShapeDtypeStruct((own_blocks * block, aux_count * orbitals), jnp.bfloat16),
        in_specs=[IN_SMEM] * 4 + [IN_VMEM] + [ANY] * len(pieces),
        out_specs=IN_VMEM,
        scratch_shapes=[
            pltpu.VMEM((blocks, block, orbitals), jnp.bfloat16),
            pltpu.VMEM((own_blocks, aux_count * block, orbitals), jnp.float32),
            pltpu.SemaphoreType.DMA((len(pieces),)),
        ],
        compiler_params=pltpu.CompilerParams(vmem_limit_bytes=32 * 1024 * 1024),
        name="half_transform",
    )(count, cols, rows, natural, integrals, *pieces)


def product(first, second):
    return lax.dot_general(first, second, (((1,), (1,)), ((), ())), preferred_element_type=jnp.float32)


def reduce_to_owner(lay, partial, owner, order):
    terms = [partial]
    done = 0
    for step, bit in enumerate(order):
        total = functools.reduce(lambda x, y: x + y.astype(jnp.float32), terms)

        def where(a, z, c, bit=bit, done=done):
            own = owner(z, c)
            if own is None or (a ^ own) & done or not (a ^ own) >> bit & 1:
                return None
            return (a ^ (1 << bit), z, c)

        terms.append(lay.send(total.astype(jnp.bfloat16), where))
        done |= 1 << bit
    return terms


def local(lay, integrals, coefficients, pair_rows, pair_cols, pair_count, row_blocks):
    aux_count, slots, block, _ = integrals.shape
    block_total = row_blocks.shape[0]
    own_blocks = block_total // lay.occ
    width = own_blocks * block
    orbitals = coefficients.shape[1]
    planes = lay.planes
    a = lax.axis_index("aux")
    occ_index = lax.axis_index("occ")
    z, c = occ_index // CORES, occ_index % CORES

    share = min(lay.aux, own_blocks)
    part = own_blocks // share
    blocks = coefficients.reshape(own_blocks, block, orbitals)
    mine = lax.dynamic_slice_in_dim(blocks, (a % share) * part, part, 0)
    far = [lay.send(mine, lambda a_, z_, c_, d=d: (a_, z_ ^ d, c_)) for d in range(1, planes)]
    far = jnp.concatenate(far, axis=0)
    spread = [far] + [lay.send(far, lambda a_, z_, c_, k=k: (a_ ^ k, z_, c_)) for k in range(1, share)]
    other = lambda v: lay.send(v, lambda a_, z_, c_: (a_, z_, 1 - c_))
    pieces = [blocks, other(blocks)]
    for piece in spread:
        pieces += [piece, other(piece)]
    half = half_transform(lay, share, own_blocks, integrals, pieces, pair_cols, pair_rows, pair_count, row_blocks)

    out_blocks = block_total * block // lay.aux // width
    x_first, y_first = tuple(range(lay.bits)), tuple(reversed(range(lay.bits)))
    entries = []

    def arrived(held, plane_of):
        def owner(z_, c_):
            plane = plane_of(z_)
            return None if plane is None else (plane * CORES + c_) // out_blocks

        same = reduce_to_owner(lay, product(held, half), owner, x_first)
        cross = reduce_to_owner(lay, product(other(held), half), lambda z_, c_: owner(z_, 1 - c_), y_first)
        entries.append((plane_of, same, cross))

    arrived(half, lambda z_: z_)
    up = down = half
    for s in range(1, planes):
        up = lay.send(up, lambda a_, z_, c_: (a_, z_ + 1, c_) if z_ + 1 < planes else None)
        down = lay.send(down, lambda a_, z_, c_: (a_, z_ - 1, c_) if z_ > 0 else None)
        below = lambda z_, s=s: z_ - s if z_ >= s else None
        above = lambda z_, s=s: z_ + s if z_ + s < planes else None
        if 2 * s < planes:
            arrived(up, below)
            arrived(down, above)
        else:
            both = jnp.where(z >= s, up, down)
            arrived(both, lambda z_, below=below, above=above: below(z_) if above(z_) is None else above(z_))

    results = []
    for t in range(out_blocks):
        row = a * out_blocks + t
        index = jnp.int32(0)
        branches = []
        for plane_of, same, cross in entries:
            plane = jnp.int32(-1)
            for z_ in range(planes):
                if plane_of(z_) is not None:
                    plane = jnp.where(z == z_, plane_of(z_), plane)
            for terms, core in ((same, c), (cross, 1 - c)):
                index = jnp.where(plane * CORES + core == row, len(branches), index)
                branches.append(lambda terms=terms: functools.reduce(lambda x, y: x + y.astype(jnp.float32), terms))
        results.append(lax.switch(index, branches))
    return jnp.concatenate(results, axis=0) if out_blocks > 1 else results[0]


def solution(mesh):
    lay = Layout(mesh.shape["aux"], mesh.shape["occ"])
    return jax.shard_map(
        functools.partial(local, lay),
        mesh=mesh,
        in_specs=(
            P("aux", "occ", None, None),
            P("occ", None),
            P("aux", "occ"),
            P("aux", "occ"),
            P("aux", "occ"),
            P(),
        ),
        out_specs=P("aux", "occ"),
        check_vma=False,
    )
```

```python
import functools
import math

import jax
import jax.numpy as jnp
from jax import lax
from jax.experimental import pallas as pl
from jax.experimental.pallas import tpu as pltpu
from jax.sharding import PartitionSpec as P

AXES = ("aux", "occ")
CORES = 2
VMEM_LIMIT = 24 * 1024 * 1024
ANY = pl.BlockSpec(memory_space=pl.ANY)
IN_HBM = pl.BlockSpec(memory_space=pltpu.HBM)
IN_VMEM = pl.BlockSpec(memory_space=pltpu.VMEM)


class Layout:
    def __init__(self, aux, occ):
        self.aux, self.occ, self.planes = aux, occ, occ // CORES
        self.bits = int(math.log2(aux))

    def send(self, value, where):
        pairs = []
        for a in range(self.aux):
            for z in range(self.planes):
                for c in range(CORES):
                    to = where(a, z, c)
                    if to is not None:
                        pairs.append((a * self.occ + z * CORES + c, to[0] * self.occ + to[1] * CORES + to[2]))
        return lax.ppermute(value, AXES, pairs)


def half_kernel(lay, share, sources, mirrored, count_ref, cols_ref, rows_ref, natural_ref, integrals_ref, *refs):
    pieces, (out_ref, coeff, ints, total, count, cols, rows, natural, found, listed, *sems) = (
        refs[:sources],
        refs[sources:],
    )
    sems, piece_sems = sems
    own_blocks = total.shape[0]
    part = own_blocks // share
    small = [
        pltpu.make_async_copy(source, target, sems.at[n])
        for n, (source, target) in enumerate(
            ((count_ref, count), (cols_ref, cols), (rows_ref, rows), (natural_ref, natural), (integrals_ref, ints))
        )
    ]
    copies = []
    start = 0
    for n, piece in enumerate(pieces):
        size = piece.shape[0]
        copies.append(pltpu.make_async_copy(piece, coeff.at[pl.ds(start, size)], piece_sems.at[n]))
        start += size
    for copy in small + copies:
        copy.start()
    total[...] = jnp.zeros_like(total)
    for copy in small + copies:
        copy.wait()
    aux_count, slots, block, _ = ints.shape
    orbitals = coeff.shape[2]
    occ_index = lax.axis_index("occ")
    z, c = occ_index // CORES, occ_index % CORES
    a = lax.axis_index("aux")
    k = a % share

    for row in range(own_blocks):
        found[row] = 0

    def enter(slot, carry):
        row = rows[0, slot]
        at = found[row]
        listed[row, at] = slot
        found[row] = at + 1
        return carry

    lax.fori_loop(0, count[0, 0], enter, 0)

    def coeff_block(slot):
        source = natural[cols[0, slot]]
        owner, inner = source // own_blocks, source % own_blocks
        z_off, c_off = (owner // CORES) ^ z, (owner % CORES) ^ c
        k_off, in_part = (inner // part) ^ k, inner % part
        near = c_off * own_blocks + inner
        base = jnp.int32(0)
        start = CORES * own_blocks
        for group in plane_groups(lay.planes):
            inside = (z_off >= group[0]) & (z_off <= group[-1])
            at = start + ((k_off * CORES + c_off) * len(group) + z_off - group[0]) * part + in_part
            base = jnp.where(inside, at, base)
            start += share * CORES * len(group) * part
        return coeff[jnp.where(z_off == 0, near, base)]

    def ints_block(slot):
        return jnp.concatenate([ints[p, slot] for p in range(aux_count)], axis=0)

    for row in range(own_blocks):
        number = found[row]
        place = row ^ a if mirrored else row

        def add_two(step, carry, row=row, number=number, place=place):
            one = listed[row, 2 * step]
            paired = 2 * step + 1 < number
            two = jnp.where(paired, listed[row, jnp.where(paired, 2 * step + 1, 2 * step)], one)
            second = ints_block(two)
            left = jnp.concatenate([ints_block(one), jnp.where(paired, second, jnp.zeros_like(second))], axis=1)
            right = jnp.concatenate([coeff_block(one), coeff_block(two)], axis=0)
            total[place] += jnp.dot(left, right, preferred_element_type=jnp.float32)
            return carry

        lax.fori_loop(0, (number + 1) // 2, add_two, 0)
    for row in range(own_blocks):
        for p in range(aux_count):
            out_ref[pl.ds(row * block, block), pl.ds(p * orbitals, orbitals)] = total[
                row, pl.ds(p * block, block), :
            ].astype(jnp.bfloat16)


def plane_groups(planes):
    return [list(range(1, 2)), list(range(2, planes))] if planes > 2 else [list(range(1, planes))]


def half_transform(lay, share, mirrored, own_blocks, integrals, pieces, cols, rows, count, natural):
    aux_count, slots, block, _ = integrals.shape
    orbitals = pieces[0].shape[2]
    blocks = sum(piece.shape[0] for piece in pieces)
    return pl.pallas_call(
        functools.partial(half_kernel, lay, share, len(pieces), mirrored),
        out_shape=jax.ShapeDtypeStruct((own_blocks * block, aux_count * orbitals), jnp.bfloat16),
        in_specs=[IN_HBM] * 5 + [ANY] * len(pieces),
        out_specs=IN_VMEM,
        scratch_shapes=[
            pltpu.VMEM((blocks, block, orbitals), jnp.bfloat16),
            pltpu.VMEM(integrals.shape, integrals.dtype),
            pltpu.VMEM((own_blocks, aux_count * block, orbitals), jnp.float32),
            pltpu.SMEM(count.shape, count.dtype),
            pltpu.SMEM(cols.shape, cols.dtype),
            pltpu.SMEM(rows.shape, rows.dtype),
            pltpu.SMEM(natural.shape, natural.dtype),
            pltpu.SMEM((own_blocks,), jnp.int32),
            pltpu.SMEM((own_blocks, slots), jnp.int32),
            pltpu.SemaphoreType.DMA((5,)),
            pltpu.SemaphoreType.DMA((len(pieces),)),
        ],
        compiler_params=pltpu.CompilerParams(vmem_limit_bytes=VMEM_LIMIT),
        name="half_transform",
    )(count, cols, rows, natural, integrals, *pieces)


def product(first, second):
    return lax.dot_general(first, second, (((1,), (1,)), ((), ())), preferred_element_type=jnp.float32)


def reduce_to_owner(lay, partial, owner, order):
    terms = [partial]
    done = 0
    for step, bit in enumerate(order):
        total = functools.reduce(lambda x, y: x + y.astype(jnp.float32), terms)

        def where(a, z, c, bit=bit, done=done):
            own = owner(z, c)
            if own is None or (a ^ own) & done or not (a ^ own) >> bit & 1:
                return None
            return (a ^ (1 << bit), z, c)

        terms.append(lay.send(total.astype(jnp.bfloat16), where))
        done |= 1 << bit
    return terms


ROWS = (((1,), (1,)), ((), ()))


def dot_rows(first, second):
    return lax.dot_general(first, second, ROWS, preferred_element_type=jnp.float32)


def plane_rows(held, s, k):
    per_core = len(held) // CORES
    whole, near, *rest = held[s * per_core : (s + 1) * per_core]
    if k == 0:
        return [whole[...].reshape(-1, whole.shape[2])]
    return [near[k - 1], rest[k - 1][...].reshape(-1, near.shape[2])]


def pair_kernel(distances, *refs):
    firsts, laters = refs[:distances], refs[distances : 2 * distances]
    held, outs = refs[2 * distances : -distances], refs[-distances:]
    n = firsts[0].shape[0]
    count = laters[0].shape[0] + 1
    quarters = [jnp.concatenate([first[...] for first in firsts], axis=0)]
    quarters += [jnp.concatenate([later[k] for later in laters], axis=0) for k in range(count - 1)]
    for s in range(CORES):
        start = s * count * n
        lower = upper = None
        for k in range(count):
            parts = [dot_rows(part, quarters[k]) for part in plane_rows(held, s, k)]
            if k == 0:
                lower, upper = parts[0][:n], parts[0][n:]
            else:
                lower, upper = lower + parts[0], upper + parts[1]
        for d, out in enumerate(outs):
            out[pl.ds(start, n), :] = lower[:, d * n : (d + 1) * n].astype(jnp.bfloat16)
            out[pl.ds(start + n, (count - 1) * n), :] = upper[:, d * n : (d + 1) * n].astype(jnp.bfloat16)


def pair_blocks(firsts, laters, held):
    count, n, _ = held[0].shape
    distances = len(firsts)
    shape = jax.ShapeDtypeStruct((CORES * count * n, n), jnp.bfloat16)
    return pl.pallas_call(
        functools.partial(pair_kernel, distances),
        out_shape=[shape] * distances,
        in_specs=[IN_VMEM] * (2 * distances + len(held)),
        out_specs=[IN_VMEM] * distances,
        compiler_params=pltpu.CompilerParams(vmem_limit_bytes=VMEM_LIMIT),
        name="pair_blocks",
    )(*firsts, *laters, *held)


def own_kernel(*refs):
    *held, _, out_ref = refs
    count, n, _ = held[0].shape
    a = lax.axis_index("aux")
    occ_index = lax.axis_index("occ")
    z, c = occ_index // CORES, occ_index % CORES

    @pl.when(a == z)
    def _():
        for s in range(CORES):
            core = c if s == 0 else 1 - c
            total = None
            for k in range(count):
                own = jnp.concatenate(plane_rows(held, 0, k), axis=0)
                value = jnp.concatenate([dot_rows(part, own) for part in plane_rows(held, s, k)], axis=0)
                total = value if total is None else total + value
            for m in range(count):
                row = pl.multiple_of(core * count * n + (a ^ m) * n, n)
                for col in range(count):
                    out_ref[pl.ds(row, n), pl.ds(pl.multiple_of((a ^ col) * n, n), n)] = total[
                        m * n : (m + 1) * n, col * n : (col + 1) * n
                    ]


def own_block(held, earlier):
    count, n, _ = held[0].shape
    return pl.pallas_call(
        own_kernel,
        out_shape=jax.ShapeDtypeStruct((CORES * count * n, count * n), jnp.float32),
        in_specs=[IN_VMEM] * len(held) + [ANY],
        out_specs=IN_VMEM,
        compiler_params=pltpu.CompilerParams(vmem_limit_bytes=VMEM_LIMIT),
        name="own_block",
    )(*held, earlier)


def place_kernel(*refs):
    *quarters, crossed_ref, own_ref, out_ref = refs
    count = len(quarters)
    n = quarters[0].shape[1]
    width = count * n
    a = lax.axis_index("aux")
    occ_index = lax.axis_index("occ")
    z, c = occ_index // CORES, occ_index % CORES
    apart = lax.rem(a - z + count, count)

    def tile(row, col, value):
        out_ref[pl.ds(pl.multiple_of(row, n), n), pl.ds(pl.multiple_of(col, n), n)] = value

    @pl.when(apart == 0)
    def _():
        out_ref[...] = own_ref[...]

    @pl.when((apart > 0) & (apart <= count // 2))
    def _():
        for k, quarter in enumerate(quarters):
            for m in range(count):
                col, rows = (a ^ k ^ m) * n, pl.ds(m * n, n)
                tile(c * width + (a ^ k) * n, col, quarter[rows, :].astype(jnp.float32).T)
                tile((1 - c) * width + (a ^ k) * n, col, crossed_ref[k, rows, :].astype(jnp.float32).T)

    @pl.when(apart > count // 2)
    def _():
        for k, quarter in enumerate(quarters):
            for s in range(CORES):
                core = c if s == 0 else 1 - c
                for m in range(count):
                    value = quarter[pl.ds((s * count + m) * n, n), :].astype(jnp.float32)
                    tile(core * width + (a ^ k ^ m) * n, (a ^ k) * n, value)


def place_blocks(quarters, crossed, out):
    return pl.pallas_call(
        place_kernel,
        out_shape=jax.ShapeDtypeStruct(out.shape, out.dtype),
        in_specs=[IN_VMEM] * (len(quarters) + 2),
        out_specs=IN_VMEM,
        compiler_params=pltpu.CompilerParams(vmem_limit_bytes=VMEM_LIMIT),
        name="place_blocks",
    )(*quarters, crossed, out)


def after(value, *done):
    return lax.optimization_barrier((value, *done))[0]


def mirrored_exchange(lay, half):
    count, n, _ = half.shape
    a = lax.axis_index("aux")
    z = lax.axis_index("occ") // CORES
    others = range(1, count)
    other = lambda v: lay.send(v, lambda a_, z_, c_: (a_, z_, 1 - c_))
    toward = lambda v, k: lay.send(v, lambda a_, z_, c_: (a_ ^ k, z_, c_))
    below = lambda v: lay.send(v, lambda a_, z_, c_: (a_, (z_ - 1) % count, c_))

    first, later = [half[0]], []
    near = jnp.stack([toward(half[k], k) for k in others])
    for d in range(1, count // 2 + 1):
        first.append(below(first[-1]))
        later.append(below(after(later[-1] if later else near, first[-1])))
    rest = [toward(after(jnp.stack([half[k ^ m] for m in others]), near, first[1]), k) for k in others]
    own = [half, near] + rest
    held = own + [other(v) for v in own[:-1]] + [other(after(own[-1], later[-1]))]

    blocks = pair_blocks(first[1:], later, held)
    apart = dict(enumerate(blocks, 1))
    for d in range(1, (count + 1) // 2):
        apart[count - d] = lay.send(apart[d], lambda a_, z_, c_: (a_, (z_ + d) % count, c_))
    out = own_block(held, blocks[0])
    apart[count - 1] = after(apart[count - 1], out)

    quarters = []
    for k in range(count):
        distance = lax.rem((a ^ k) - z + count, count)
        value = apart[1]
        for d in range(2, count):
            value = jnp.where(distance == d, apart[d], value)
        if k:
            value = lay.send(value, lambda a_, z_, c_: (a_ ^ k, z_, c_) if a_ ^ k != z_ else None)
        quarters.append(value)
    crossed = other(jnp.stack([q[count * n :] for q in quarters]))
    return place_blocks(quarters, crossed, out)


def local(lay, integrals, coefficients, pair_rows, pair_cols, pair_count, row_blocks):
    aux_count, slots, block, _ = integrals.shape
    block_total = row_blocks.shape[0]
    own_blocks = block_total // lay.occ
    width = own_blocks * block
    orbitals = coefficients.shape[1]
    planes = lay.planes
    a = lax.axis_index("aux")
    occ_index = lax.axis_index("occ")
    z, c = occ_index // CORES, occ_index % CORES

    share = min(lay.aux, own_blocks)
    part = own_blocks // share
    blocks = coefficients.reshape(own_blocks, block, orbitals)
    mine = lax.dynamic_slice_in_dim(blocks, (a % share) * part, part, 0)
    other = lambda v: lay.send(v, lambda a_, z_, c_: (a_, z_, 1 - c_))
    pieces = [blocks, other(blocks)]
    for group in plane_groups(planes):
        far = [lay.send(mine, lambda a_, z_, c_, d=d: (a_, z_ ^ d, c_)) for d in group]
        far = jnp.concatenate(far, axis=0) if len(far) > 1 else far[0]
        for k in range(share):
            piece = lay.send(far, lambda a_, z_, c_, k=k: (a_ ^ k, z_, c_)) if k else far
            pieces += [piece, other(piece)]
    mirrored = lay.aux == planes == own_blocks and planes % 2 == 0
    half = half_transform(lay, share, mirrored, own_blocks, integrals, pieces, pair_cols, pair_rows, pair_count, row_blocks)

    if mirrored:
        return mirrored_exchange(lay, half.reshape(own_blocks, block, -1))

    out_blocks = block_total * block // lay.aux // width
    x_first, y_first = tuple(range(lay.bits)), tuple(reversed(range(lay.bits)))
    entries = []

    def arrived(held, plane_of):
        def owner(z_, c_):
            plane = plane_of(z_)
            return None if plane is None else (plane * CORES + c_) // out_blocks

        same = reduce_to_owner(lay, product(held, half), owner, x_first)
        cross = reduce_to_owner(lay, product(other(held), half), lambda z_, c_: owner(z_, 1 - c_), y_first)
        entries.append((plane_of, same, cross))

    arrived(half, lambda z_: z_)
    up = down = half
    for s in range(1, planes):
        up = lay.send(up, lambda a_, z_, c_: (a_, z_ + 1, c_) if z_ + 1 < planes else None)
        down = lay.send(down, lambda a_, z_, c_: (a_, z_ - 1, c_) if z_ > 0 else None)
        below = lambda z_, s=s: z_ - s if z_ >= s else None
        above = lambda z_, s=s: z_ + s if z_ + s < planes else None
        if 2 * s < planes:
            arrived(up, below)
            arrived(down, above)
        else:
            both = jnp.where(z >= s, up, down)
            arrived(both, lambda z_, below=below, above=above: below(z_) if above(z_) is None else above(z_))

    results = []
    for t in range(out_blocks):
        row = a * out_blocks + t
        index = jnp.int32(0)
        branches = []
        for plane_of, same, cross in entries:
            plane = jnp.int32(-1)
            for z_ in range(planes):
                if plane_of(z_) is not None:
                    plane = jnp.where(z == z_, plane_of(z_), plane)
            for terms, core in ((same, c), (cross, 1 - c)):
                index = jnp.where(plane * CORES + core == row, len(branches), index)
                branches.append(lambda terms=terms: functools.reduce(lambda x, y: x + y.astype(jnp.float32), terms))
        results.append(lax.switch(index, branches))
    return jnp.concatenate(results, axis=0) if out_blocks > 1 else results[0]


def solution(mesh):
    lay = Layout(mesh.shape["aux"], mesh.shape["occ"])
    return jax.shard_map(
        functools.partial(local, lay),
        mesh=mesh,
        in_specs=(
            P("aux", "occ", None, None),
            P("occ", None),
            P("aux", "occ"),
            P("aux", "occ"),
            P("aux", "occ"),
            P(),
        ),
        out_specs=P("aux", "occ"),
        check_vma=False,
    )
```

```python
import functools
import math

import jax
import jax.numpy as jnp
from jax import lax
from jax.experimental import pallas as pl
from jax.experimental.pallas import tpu as pltpu
from jax.sharding import PartitionSpec as P

AXES = ("aux", "occ")
CORES = 2
VMEM_LIMIT = 12 * 1024 * 1024
VMEM_MOST = 60 * 1024 * 1024
ANY = pl.BlockSpec(memory_space=pl.ANY)
IN_SMEM = pl.BlockSpec(memory_space=pltpu.SMEM)
IN_VMEM = pl.BlockSpec(memory_space=pltpu.VMEM)


class Layout:
    def __init__(self, aux, occ):
        self.aux, self.occ, self.planes = aux, occ, occ // CORES
        self.bits = int(math.log2(aux))

    def send(self, value, where):
        pairs = []
        for a in range(self.aux):
            for z in range(self.planes):
                for c in range(CORES):
                    to = where(a, z, c)
                    if to is not None:
                        pairs.append((a * self.occ + z * CORES + c, to[0] * self.occ + to[1] * CORES + to[2]))
        return lax.ppermute(value, AXES, pairs)


def half_kernel(lay, share, sources, mirrored, meta, ints, *refs):
    pieces, (*outs, coeff, total, found, listed) = refs[:sources], refs[sources:]
    own_blocks = total.shape[0]
    part = own_blocks // share
    start = 0
    for piece in pieces:
        coeff[pl.ds(start, piece.shape[0])] = piece[...]
        start += piece.shape[0]
    aux_count, slots, block, _ = ints.shape
    cols_at, rows_at, natural_at = 1, 1 + slots, 1 + 2 * slots
    total[...] = jnp.zeros_like(total)
    orbitals = coeff.shape[2]
    occ_index = lax.axis_index("occ")
    z, c = occ_index // CORES, occ_index % CORES
    a = lax.axis_index("aux")
    k = a % share

    for row in range(own_blocks):
        found[row] = 0

    def enter(slot, carry):
        row = meta[0, rows_at + slot]
        at = found[row]
        listed[row, at] = slot
        found[row] = at + 1
        return carry

    lax.fori_loop(0, meta[0, 0], enter, 0)

    def coeff_block(slot):
        source = meta[0, natural_at + meta[0, cols_at + slot]]
        owner, inner = source // own_blocks, source % own_blocks
        z_off, c_off = (owner // CORES) ^ z, (owner % CORES) ^ c
        k_off, in_part = (inner // part) ^ k, inner % part
        near = c_off * own_blocks + inner
        base = jnp.int32(0)
        start = CORES * own_blocks
        for group in plane_groups(lay.planes):
            inside = (z_off >= group[0]) & (z_off <= group[-1])
            at = start + ((k_off * CORES + c_off) * len(group) + z_off - group[0]) * part + in_part
            base = jnp.where(inside, at, base)
            start += share * CORES * len(group) * part
        return coeff[jnp.where(z_off == 0, near, base)]

    def ints_block(slot):
        return jnp.concatenate([ints[p, slot] for p in range(aux_count)], axis=0)

    for row in range(own_blocks):
        number = found[row]
        place = row ^ a if mirrored else row

        def add_two(step, carry, row=row, number=number, place=place):
            one = listed[row, 2 * step]
            paired = 2 * step + 1 < number
            two = jnp.where(paired, listed[row, jnp.where(paired, 2 * step + 1, 2 * step)], one)
            second = ints_block(two)
            left = jnp.concatenate([ints_block(one), jnp.where(paired, second, jnp.zeros_like(second))], axis=1)
            right = jnp.concatenate([coeff_block(one), coeff_block(two)], axis=0)
            total[place] += jnp.dot(left, right, preferred_element_type=jnp.float32)
            return carry

        lax.fori_loop(0, (number + 1) // 2, add_two, 0)
    for row in range(own_blocks):
        for p in range(aux_count):
            value = total[row, pl.ds(p * block, block), :].astype(jnp.bfloat16)
            columns = pl.ds(p * orbitals, orbitals)
            outs[0][row, :, columns] = value
            if mirrored:
                outs[1 + row][0, :, columns] = value
                for place in range(1, own_blocks):
                    if place != row:
                        outs[own_blocks + place][(place ^ row) - 1, :, columns] = value


def plane_groups(planes):
    return [list(range(1, 2)), list(range(2, planes))] if planes > 2 else [list(range(1, planes))]


def half_transform(lay, share, mirrored, own_blocks, integrals, pieces, meta):
    aux_count, slots, block, _ = integrals.shape
    orbitals = pieces[0].shape[2]
    blocks = sum(piece.shape[0] for piece in pieces)
    sizes = [own_blocks]
    if mirrored:
        sizes += [1] * own_blocks + [own_blocks - 1] * (own_blocks - 1)
    return pl.pallas_call(
        functools.partial(half_kernel, lay, share, len(pieces), mirrored),
        out_shape=[jax.ShapeDtypeStruct((size, block, aux_count * orbitals), jnp.bfloat16) for size in sizes],
        in_specs=[IN_SMEM] + [IN_VMEM] * (1 + len(pieces)),
        out_specs=[IN_VMEM] * len(sizes),
        scratch_shapes=[
            pltpu.VMEM((blocks, block, orbitals), jnp.bfloat16),
            pltpu.VMEM((own_blocks, aux_count * block, orbitals), jnp.float32),
            pltpu.SMEM((own_blocks,), jnp.int32),
            pltpu.SMEM((own_blocks, slots), jnp.int32),
        ],
        compiler_params=pltpu.CompilerParams(vmem_limit_bytes=VMEM_LIMIT),
        name="half_transform",
    )(meta, integrals, *pieces)


ROWS = (((1,), (1,)), ((), ()))


def dot_rows(first, second):
    return lax.dot_general(first, second, ROWS, preferred_element_type=jnp.float32)


STEPS = ([[0], [1, 2, 3]], [[0], [1, 2, 3]])
HELD = 5


def core_parts(held, s, k):
    whole, near, *rest = held[s * HELD : (s + 1) * HELD]
    depth = whole.shape[2]
    if k == 0:
        return [whole[...].reshape(-1, depth)]
    return [near[k - 1], rest[k - 1][...].reshape(-1, depth)]


def pair_kernel(*refs):
    held, outs = refs[-len(STEPS) - CORES * HELD : -len(STEPS)], refs[-len(STEPS) :]
    count, n, _ = held[0].shape
    quarters = [[] for _ in range(count)]
    at = 0
    for step in STEPS:
        for group in step:
            for place, k in enumerate(group):
                quarters[k].append(refs[at][place])
            at += 1
    quarters = [jnp.concatenate(parts, axis=0) for parts in quarters]
    for s in range(CORES):
        start = s * count * n
        lower = upper = None
        for k in range(count):
            parts = [dot_rows(part, quarters[k]) for part in core_parts(held, s, k)]
            if k == 0:
                lower, upper = parts[0][:n], parts[0][n:]
            else:
                lower, upper = lower + parts[0], upper + parts[1]
        for d, out in enumerate(outs):
            out[pl.ds(start, n), :] = lower[:, d * n : (d + 1) * n].astype(jnp.bfloat16)
            out[pl.ds(start + n, (count - 1) * n), :] = upper[:, d * n : (d + 1) * n].astype(jnp.bfloat16)


def pair_blocks(rows, held):
    count, n, _ = held[0].shape
    flat = [part for parts in rows for part in parts]
    shape = jax.ShapeDtypeStruct((CORES * count * n, n), jnp.bfloat16)
    return pl.pallas_call(
        pair_kernel,
        out_shape=[shape] * len(STEPS),
        in_specs=[IN_VMEM] * (len(flat) + len(held)),
        out_specs=[IN_VMEM] * len(STEPS),
        compiler_params=pltpu.CompilerParams(vmem_limit_bytes=VMEM_LIMIT),
        name="pair_blocks",
    )(*flat, *held)


def own_kernel(*refs):
    *held, _, out_ref, plane, sems = refs
    _, count, rows, depth = plane.shape
    n = rows // count
    a = lax.axis_index("aux")
    occ_index = lax.axis_index("occ")
    z, c = occ_index // CORES, occ_index % CORES

    def moves(s, k):
        whole, near, *rest = held[s * HELD : (s + 1) * HELD]
        parts = [(whole if k == 0 else rest[k - 1]).at[m] for m in range(count if k == 0 else count - 1)]
        if k:
            parts = [near.at[k - 1]] + parts
        return [pltpu.make_async_copy(x, plane.at[s, k, pl.ds(m * n, n)], sems.at[s, k, m]) for m, x in enumerate(parts)]

    @pl.when(a == z)
    def _():
        copies = {(s, k): moves(s, k) for s in range(CORES) for k in range(count)}
        for parts in copies.values():
            for copy in parts:
                copy.start()
        for s in range(CORES):
            core = c if s == 0 else 1 - c
            total = None
            for k in range(count):
                for copy in copies[s, k]:
                    copy.wait()
                value = dot_rows(plane[s, k], plane[0, k])
                total = value if total is None else total + value
            for m in range(count):
                row = pl.multiple_of(core * rows + (a ^ m) * n, n)
                for col in range(count):
                    out_ref[pl.ds(row, n), pl.ds(pl.multiple_of((a ^ col) * n, n), n)] = total[
                        m * n : (m + 1) * n, col * n : (col + 1) * n
                    ]


def own_block(held, earlier):
    count, n, depth = held[0].shape
    return pl.pallas_call(
        own_kernel,
        out_shape=jax.ShapeDtypeStruct((CORES * count * n, count * n), jnp.float32),
        in_specs=[ANY] * (len(held) + 1),
        out_specs=IN_VMEM,
        scratch_shapes=[
            pltpu.VMEM((CORES, count, count * n, depth), jnp.bfloat16),
            pltpu.SemaphoreType.DMA((CORES, count, count)),
        ],
        compiler_params=pltpu.CompilerParams(vmem_limit_bytes=VMEM_MOST),
        name="own_block",
    )(*held, earlier)


def place_kernel(*refs):
    *quarters, own_ref, out_ref = refs
    count = len(quarters)
    n = quarters[0].shape[1]
    width = count * n
    a = lax.axis_index("aux")
    occ_index = lax.axis_index("occ")
    z, c = occ_index // CORES, occ_index % CORES
    apart = lax.rem(a - z + count, count)

    def tile(row, col, value):
        out_ref[pl.ds(pl.multiple_of(row, n), n), pl.ds(pl.multiple_of(col, n), n)] = value

    @pl.when(apart == 0)
    def _():
        out_ref[...] = own_ref[...]

    @pl.when((apart > 0) & (apart <= count // 2))
    def _():
        for k, quarter in enumerate(quarters):
            for s in range(CORES):
                row = (c if s == 0 else 1 - c) * width + (a ^ k) * n
                for m in range(count):
                    value = quarter[pl.ds((s * count + m) * n, n), :].astype(jnp.float32)
                    tile(row, (a ^ k ^ m) * n, value.T)

    @pl.when(apart > count // 2)
    def _():
        for k, quarter in enumerate(quarters):
            for s in range(CORES):
                core = c if s == 0 else 1 - c
                for m in range(count):
                    value = quarter[pl.ds((s * count + m) * n, n), :].astype(jnp.float32)
                    tile(core * width + (a ^ k ^ m) * n, (a ^ k) * n, value)


def place_blocks(quarters, out):
    return pl.pallas_call(
        place_kernel,
        out_shape=jax.ShapeDtypeStruct(out.shape, out.dtype),
        in_specs=[IN_VMEM] * (len(quarters) + 1),
        out_specs=IN_VMEM,
        compiler_params=pltpu.CompilerParams(vmem_limit_bytes=VMEM_LIMIT),
        name="place_blocks",
    )(*quarters, out)


def after(value, *done):
    return lax.optimization_barrier((value, *done))[0]


def mirrored_exchange(lay, half, *sent):
    count, n, _ = half.shape
    a = lax.axis_index("aux")
    z = lax.axis_index("occ") // CORES
    others = range(1, count)
    other = lambda v: lay.send(v, lambda a_, z_, c_: (a_, z_, 1 - c_))
    toward = lambda v, k: lay.send(v, lambda a_, z_, c_: (a_ ^ k, z_, c_))
    below = lambda v: lay.send(v, lambda a_, z_, c_: (a_, (z_ - 1) % count, c_))

    near = jnp.concatenate([toward(sent[k], k) for k in others])
    first, later = [sent[0]], [near]
    for _ in STEPS:
        first.append(below(first[-1]))
    for d in range(len(STEPS)):
        later.append(below(after(later[-1], first[-1]) if d == 0 else later[-1]))
    rest = [toward(after(sent[count - 1 + k], near), k) for k in others]
    own = [half, near] + rest
    held = own + [other(v) for v in own[:-1]] + [other(after(own[-1], later[-1]))]

    ahead = pair_blocks(list(zip(first[1:], later[1:])), held)
    mirror = lay.send(ahead[0], lambda a_, z_, c_: (a_, (z_ + 1) % count, c_))
    out = own_block(held, ahead[1])
    width = count * n
    ahead = [jnp.concatenate([v[:width], other(v[width:])]) for v in ahead]
    apart = {1: ahead[0], 2: ahead[1], 3: after(mirror, out)}

    quarters = []
    for k in range(count):
        distance = lax.rem((a ^ k) - z + count, count)
        value = apart[1]
        for d in range(2, count):
            value = jnp.where(distance == d, apart[d], value)
        if k:
            value = lay.send(value, lambda a_, z_, c_: (a_ ^ k, z_, c_) if a_ ^ k != z_ else None)
        quarters.append(value)
    return place_blocks(quarters, out)


def product(first, second):
    return lax.dot_general(first, second, (((1,), (1,)), ((), ())), preferred_element_type=jnp.float32)


def reduce_to_owner(lay, partial, owner, order):
    terms = [partial]
    done = 0
    for step, bit in enumerate(order):
        total = functools.reduce(lambda x, y: x + y.astype(jnp.float32), terms)

        def where(a, z, c, bit=bit, done=done):
            own = owner(z, c)
            if own is None or (a ^ own) & done or not (a ^ own) >> bit & 1:
                return None
            return (a ^ (1 << bit), z, c)

        terms.append(lay.send(total.astype(jnp.bfloat16), where))
        done |= 1 << bit
    return terms


def local(lay, integrals, coefficients, pair_rows, pair_cols, pair_count, row_blocks):
    aux_count, slots, block, _ = integrals.shape
    block_total = row_blocks.shape[0]
    own_blocks = block_total // lay.occ
    width = own_blocks * block
    orbitals = coefficients.shape[1]
    planes = lay.planes
    a = lax.axis_index("aux")
    occ_index = lax.axis_index("occ")
    z, c = occ_index // CORES, occ_index % CORES

    share = min(lay.aux, own_blocks)
    part = own_blocks // share
    blocks = coefficients.reshape(own_blocks, block, orbitals)
    mine = lax.dynamic_slice_in_dim(blocks, (a % share) * part, part, 0)
    other = lambda v: lay.send(v, lambda a_, z_, c_: (a_, z_, 1 - c_))
    pieces = [blocks, other(blocks)]
    meta = jnp.concatenate([v.reshape(1, -1) for v in (pair_count, pair_cols, pair_rows, row_blocks)], axis=1)
    for group in plane_groups(planes):
        far = [lay.send(mine, lambda a_, z_, c_, d=d: (a_, z_ ^ d, c_)) for d in group]
        far = jnp.concatenate(far, axis=0) if len(far) > 1 else far[0]
        for k in range(share):
            piece = lay.send(far, lambda a_, z_, c_, k=k: (a_ ^ k, z_, c_)) if k else far
            pieces += [piece, other(piece)]
    mirrored = lay.aux == planes == own_blocks == 4
    half = half_transform(lay, share, mirrored, own_blocks, integrals, pieces, meta)

    if mirrored:
        return mirrored_exchange(lay, *half)

    half = half[0].reshape(width, -1)

    out_blocks = block_total * block // lay.aux // width
    x_first, y_first = tuple(range(lay.bits)), tuple(reversed(range(lay.bits)))
    entries = []

    def arrived(held, plane_of):
        def owner(z_, c_):
            plane = plane_of(z_)
            return None if plane is None else (plane * CORES + c_) // out_blocks

        same = reduce_to_owner(lay, product(held, half), owner, x_first)
        cross = reduce_to_owner(lay, product(other(held), half), lambda z_, c_: owner(z_, 1 - c_), y_first)
        entries.append((plane_of, same, cross))

    arrived(half, lambda z_: z_)
    up = down = half
    for s in range(1, planes):
        up = lay.send(up, lambda a_, z_, c_: (a_, z_ + 1, c_) if z_ + 1 < planes else None)
        down = lay.send(down, lambda a_, z_, c_: (a_, z_ - 1, c_) if z_ > 0 else None)
        below = lambda z_, s=s: z_ - s if z_ >= s else None
        above = lambda z_, s=s: z_ + s if z_ + s < planes else None
        if 2 * s < planes:
            arrived(up, below)
            arrived(down, above)
        else:
            both = jnp.where(z >= s, up, down)
            arrived(both, lambda z_, below=below, above=above: below(z_) if above(z_) is None else above(z_))

    results = []
    for t in range(out_blocks):
        row = a * out_blocks + t
        index = jnp.int32(0)
        branches = []
        for plane_of, same, cross in entries:
            plane = jnp.int32(-1)
            for z_ in range(planes):
                if plane_of(z_) is not None:
                    plane = jnp.where(z == z_, plane_of(z_), plane)
            for terms, core in ((same, c), (cross, 1 - c)):
                index = jnp.where(plane * CORES + core == row, len(branches), index)
                branches.append(lambda terms=terms: functools.reduce(lambda x, y: x + y.astype(jnp.float32), terms))
        results.append(lax.switch(index, branches))
    return jnp.concatenate(results, axis=0) if out_blocks > 1 else results[0]


def solution(mesh):
    lay = Layout(mesh.shape["aux"], mesh.shape["occ"])
    return jax.shard_map(
        functools.partial(local, lay),
        mesh=mesh,
        in_specs=(
            P("aux", "occ", None, None),
            P("occ", None),
            P("aux", "occ"),
            P("aux", "occ"),
            P("aux", "occ"),
            P(),
        ),
        out_specs=P("aux", "occ"),
        check_vma=False,
    )
```

```python
import functools
import math

import jax
import jax.numpy as jnp
from jax import lax
from jax.experimental import pallas as pl
from jax.experimental.pallas import tpu as pltpu
from jax.sharding import PartitionSpec as P

AXES = ("aux", "occ")
CORES = 2
VMEM_LIMIT = 12 * 1024 * 1024
VMEM_MOST = 60 * 1024 * 1024
ANY = pl.BlockSpec(memory_space=pl.ANY)
IN_SMEM = pl.BlockSpec(memory_space=pltpu.SMEM)
IN_VMEM = pl.BlockSpec(memory_space=pltpu.VMEM)


class Layout:
    def __init__(self, aux, occ):
        self.aux, self.occ, self.planes = aux, occ, occ // CORES
        self.bits = int(math.log2(aux))

    def send(self, value, where):
        pairs = []
        for a in range(self.aux):
            for z in range(self.planes):
                for c in range(CORES):
                    to = where(a, z, c)
                    if to is not None:
                        pairs.append((a * self.occ + z * CORES + c, to[0] * self.occ + to[1] * CORES + to[2]))
        return lax.ppermute(value, AXES, pairs)


def half_kernel(lay, share, sources, mirrored, meta, ints, *refs):
    pieces, (*outs, coeff, total, found, listed) = refs[:sources], refs[sources:]
    own_blocks = total.shape[0]
    part = own_blocks // share
    start = 0
    for piece in pieces:
        coeff[pl.ds(start, piece.shape[0])] = piece[...]
        start += piece.shape[0]
    aux_count, slots, block, _ = ints.shape
    cols_at, rows_at, natural_at = 1, 1 + slots, 1 + 2 * slots
    total[...] = jnp.zeros_like(total)
    orbitals = coeff.shape[2]
    occ_index = lax.axis_index("occ")
    z, c = occ_index // CORES, occ_index % CORES
    a = lax.axis_index("aux")
    k = a % share

    for row in range(own_blocks):
        found[row] = 0

    def enter(slot, carry):
        row = meta[0, rows_at + slot]
        at = found[row]
        listed[row, at] = slot
        found[row] = at + 1
        return carry

    lax.fori_loop(0, meta[0, 0], enter, 0)

    def coeff_block(slot):
        source = meta[0, natural_at + meta[0, cols_at + slot]]
        owner, inner = source // own_blocks, source % own_blocks
        z_off, c_off = (owner // CORES) ^ z, (owner % CORES) ^ c
        k_off, in_part = (inner // part) ^ k, inner % part
        near = c_off * own_blocks + inner
        base = jnp.int32(0)
        start = CORES * own_blocks
        for group in plane_groups(lay.planes):
            inside = (z_off >= group[0]) & (z_off <= group[-1])
            at = start + ((k_off * CORES + c_off) * len(group) + z_off - group[0]) * part + in_part
            base = jnp.where(inside, at, base)
            start += share * CORES * len(group) * part
        return coeff[jnp.where(z_off == 0, near, base)]

    def ints_block(slot):
        return jnp.concatenate([ints[p, slot] for p in range(aux_count)], axis=0)

    for row in range(own_blocks):
        number = found[row]
        place = row ^ a if mirrored else row

        def add_two(step, carry, row=row, number=number, place=place):
            one = listed[row, 2 * step]
            paired = 2 * step + 1 < number
            two = jnp.where(paired, listed[row, jnp.where(paired, 2 * step + 1, 2 * step)], one)
            second = ints_block(two)
            left = jnp.concatenate([ints_block(one), jnp.where(paired, second, jnp.zeros_like(second))], axis=1)
            right = jnp.concatenate([coeff_block(one), coeff_block(two)], axis=0)
            total[place] += jnp.dot(left, right, preferred_element_type=jnp.float32)
            return carry

        lax.fori_loop(0, (number + 1) // 2, add_two, 0)
    for row in range(own_blocks):
        for p in range(aux_count):
            value = total[row, pl.ds(p * block, block), :].astype(jnp.bfloat16)
            columns = pl.ds(p * orbitals, orbitals)
            outs[0][row, :, columns] = value
            if mirrored:
                outs[1 + row][0, :, columns] = value
                for place in range(1, own_blocks):
                    if place != row:
                        outs[own_blocks + place][(place ^ row) - 1, :, columns] = value


def plane_groups(planes):
    return [list(range(1, 2)), list(range(2, planes))] if planes > 2 else [list(range(1, planes))]


def half_transform(lay, share, mirrored, own_blocks, integrals, pieces, meta):
    aux_count, slots, block, _ = integrals.shape
    orbitals = pieces[0].shape[2]
    blocks = sum(piece.shape[0] for piece in pieces)
    sizes = [own_blocks]
    if mirrored:
        sizes += [1] * own_blocks + [own_blocks - 1] * (own_blocks - 1)
    return pl.pallas_call(
        functools.partial(half_kernel, lay, share, len(pieces), mirrored),
        out_shape=[jax.ShapeDtypeStruct((size, block, aux_count * orbitals), jnp.bfloat16) for size in sizes],
        in_specs=[IN_SMEM] + [IN_VMEM] * (1 + len(pieces)),
        out_specs=[IN_VMEM] * len(sizes),
        scratch_shapes=[
            pltpu.VMEM((blocks, block, orbitals), jnp.bfloat16),
            pltpu.VMEM((own_blocks, aux_count * block, orbitals), jnp.float32),
            pltpu.SMEM((own_blocks,), jnp.int32),
            pltpu.SMEM((own_blocks, slots), jnp.int32),
        ],
        compiler_params=pltpu.CompilerParams(vmem_limit_bytes=VMEM_LIMIT),
        name="half_transform",
    )(meta, integrals, *pieces)


ROWS = (((1,), (1,)), ((), ()))


def dot_rows(first, second):
    return lax.dot_general(first, second, ROWS, preferred_element_type=jnp.float32)


STEPS = ([[0], [1, 2], [3]], [[0, 1, 2], [3]])
HELD = 5


def core_parts(held, s, k):
    whole, near, first, second, passed = held[s * HELD : (s + 1) * HELD]
    n, depth = whole.shape[1:]
    if k == 0:
        return [whole[...].reshape(-1, depth)]
    if k < 3:
        return [near[k - 1], (first if k == 1 else second)[...].reshape(-1, depth)]
    rows = [passed[0, :n], passed[1, :n], passed[0, n:], passed[1, n:]]
    return [near[k - 1], jnp.concatenate(rows, axis=0)]


def pair_kernel(*refs):
    held, outs = refs[-len(STEPS) - CORES * HELD : -len(STEPS)], refs[-len(STEPS) :]
    count, n, _ = held[0].shape
    quarters = [[] for _ in range(count)]
    at = 0
    for step in STEPS:
        for group in step:
            for place, k in enumerate(group):
                quarters[k].append(refs[at][place])
            at += 1
    quarters = [jnp.concatenate(parts, axis=0) for parts in quarters]
    for s in range(CORES):
        start = s * count * n
        lower = upper = None
        for k in range(count):
            parts = [dot_rows(part, quarters[k]) for part in core_parts(held, s, k)]
            if k == 0:
                lower, upper = parts[0][:n], parts[0][n:]
            else:
                lower, upper = lower + parts[0], upper + parts[1]
        for d, out in enumerate(outs):
            out[pl.ds(start, n), :] = lower[:, d * n : (d + 1) * n].astype(jnp.bfloat16)
            out[pl.ds(start + n, (count - 1) * n), :] = upper[:, d * n : (d + 1) * n].astype(jnp.bfloat16)


def pair_blocks(rows, held):
    count, n, _ = held[0].shape
    flat = [part for parts in rows for part in parts]
    shape = jax.ShapeDtypeStruct((CORES * count * n, n), jnp.bfloat16)
    return pl.pallas_call(
        pair_kernel,
        out_shape=[shape] * len(STEPS),
        in_specs=[IN_VMEM] * (len(flat) + len(held)),
        out_specs=[IN_VMEM] * len(STEPS),
        compiler_params=pltpu.CompilerParams(vmem_limit_bytes=VMEM_LIMIT),
        name="pair_blocks",
    )(*flat, *held)


def own_kernel(*refs):
    *held, out_ref, plane, sems = refs
    _, count, rows, depth = plane.shape
    n = rows // count
    a = lax.axis_index("aux")
    occ_index = lax.axis_index("occ")
    z, c = occ_index // CORES, occ_index % CORES

    def moves(s, k):
        whole, near, first, second, passed = held[s * HELD : (s + 1) * HELD]
        half = n // 2
        if k == 0:
            parts = [(whole.at[m], m * n, n) for m in range(count)]
        elif k < 3:
            rest = first if k == 1 else second
            parts = [(near.at[k - 1], 0, n)] + [(rest.at[m - 1], m * n, n) for m in range(1, count)]
        else:
            parts = [(near.at[k - 1], 0, n)]
            for side in range(2):
                parts.append((passed.at[side, pl.ds(0, n)], (1 + side) * n, n))
                parts.append((passed.at[side, pl.ds(n, half)], 3 * n + side * half, half))
        return [
            pltpu.make_async_copy(x, plane.at[s, k, pl.ds(start, size)], sems.at[s, k, i])
            for i, (x, start, size) in enumerate(parts)
        ]

    @pl.when(a == z)
    def _():
        copies = {(s, k): moves(s, k) for s in range(CORES) for k in range(count)}
        for parts in copies.values():
            for copy in parts:
                copy.start()
        for s in range(CORES):
            core = c if s == 0 else 1 - c
            total = None
            for k in range(count):
                for copy in copies[s, k]:
                    copy.wait()
                value = dot_rows(plane[s, k], plane[0, k])
                total = value if total is None else total + value
            for m in range(count):
                row = pl.multiple_of(core * rows + (a ^ m) * n, n)
                for col in range(count):
                    out_ref[pl.ds(row, n), pl.ds(pl.multiple_of((a ^ col) * n, n), n)] = total[
                        m * n : (m + 1) * n, col * n : (col + 1) * n
                    ]


def own_block(held):
    count, n, depth = held[0].shape
    return pl.pallas_call(
        own_kernel,
        out_shape=jax.ShapeDtypeStruct((CORES * count * n, count * n), jnp.float32),
        in_specs=[ANY] * len(held),
        out_specs=IN_VMEM,
        scratch_shapes=[
            pltpu.VMEM((CORES, count, count * n, depth), jnp.bfloat16),
            pltpu.SemaphoreType.DMA((CORES, count, count + 1)),
        ],
        compiler_params=pltpu.CompilerParams(vmem_limit_bytes=VMEM_MOST),
        name="own_block",
    )(*held)


def place_kernel(*refs):
    *quarters, own_ref, out_ref = refs
    count = len(quarters)
    n = quarters[0].shape[1]
    width = count * n
    a = lax.axis_index("aux")
    occ_index = lax.axis_index("occ")
    z, c = occ_index // CORES, occ_index % CORES
    apart = lax.rem(a - z + count, count)

    def tile(row, col, value):
        out_ref[pl.ds(pl.multiple_of(row, n), n), pl.ds(pl.multiple_of(col, n), n)] = value

    @pl.when(apart == 0)
    def _():
        out_ref[...] = own_ref[...]

    @pl.when((apart > 0) & (apart <= count // 2))
    def _():
        for k, quarter in enumerate(quarters):
            for s in range(CORES):
                row = (c if s == 0 else 1 - c) * width + (a ^ k) * n
                for m in range(count):
                    value = quarter[pl.ds((s * count + m) * n, n), :].astype(jnp.float32)
                    tile(row, (a ^ k ^ m) * n, value.T)

    @pl.when(apart > count // 2)
    def _():
        for k, quarter in enumerate(quarters):
            for s in range(CORES):
                core = c if s == 0 else 1 - c
                for m in range(count):
                    value = quarter[pl.ds((s * count + m) * n, n), :].astype(jnp.float32)
                    tile(core * width + (a ^ k ^ m) * n, (a ^ k) * n, value)


def place_blocks(quarters, out):
    return pl.pallas_call(
        place_kernel,
        out_shape=jax.ShapeDtypeStruct(out.shape, out.dtype),
        in_specs=[IN_VMEM] * (len(quarters) + 1),
        out_specs=IN_VMEM,
        compiler_params=pltpu.CompilerParams(vmem_limit_bytes=VMEM_LIMIT),
        name="place_blocks",
    )(*quarters, out)


def after(value, *done):
    return lax.optimization_barrier((value, *done))[0]


def mirrored_exchange(lay, half, *sent):
    count, n, _ = half.shape
    a = lax.axis_index("aux")
    z = lax.axis_index("occ") // CORES
    others = range(1, count)
    other = lambda v: lay.send(v, lambda a_, z_, c_: (a_, z_, 1 - c_))
    toward = lambda v, k: lay.send(v, lambda a_, z_, c_: (a_ ^ k, z_, c_))
    below = lambda v: lay.send(v, lambda a_, z_, c_: (a_, (z_ - 1) % count, c_))

    quarter = {k: toward(sent[k], k) for k in others}
    beside = jnp.concatenate([quarter[1], quarter[2]])
    begun = below(sent[0])
    rows = [[begun, below(beside), below(after(quarter[3], begun))]]
    rows.append([below(jnp.concatenate(rows[0][:2])), below(rows[0][2])])
    near = jnp.concatenate([quarter[k] for k in others])
    crossed = [other(half), other(near)]
    first, second = (toward(after(sent[count - 1 + k], near, begun, crossed[0]), k) for k in (1, 2))
    up = toward(after(jnp.concatenate([first[2], first[0, : n // 2]]), crossed[1]), 2)
    over = toward(after(jnp.concatenate([second[2], second[1, n // 2 :]]), rows[0][2]), 1)
    passed = jnp.stack([up, over])
    crossed += [other(first), other(second), other(after(passed, *rows[-1]))]
    held = [half, near, first, second, passed] + crossed

    ahead = pair_blocks(rows, held)
    mirror = lay.send(ahead[0], lambda a_, z_, c_: (a_, (z_ + 1) % count, c_))
    out = own_block(held)
    width = count * n
    ahead = [jnp.concatenate([v[:width], other(v[width:])]) for v in ahead]
    apart = {1: ahead[0], 2: after(ahead[1], out), 3: mirror}

    quarters = []
    for k in range(count):
        distance = lax.rem((a ^ k) - z + count, count)
        value = apart[1]
        for d in range(2, count):
            value = jnp.where(distance == d, apart[d], value)
        if k:
            value = lay.send(value, lambda a_, z_, c_: (a_ ^ k, z_, c_) if a_ ^ k != z_ else None)
        quarters.append(value)
    return place_blocks(quarters, out)


def product(first, second):
    return lax.dot_general(first, second, (((1,), (1,)), ((), ())), preferred_element_type=jnp.float32)


def reduce_to_owner(lay, partial, owner, order):
    terms = [partial]
    done = 0
    for step, bit in enumerate(order):
        total = functools.reduce(lambda x, y: x + y.astype(jnp.float32), terms)

        def where(a, z, c, bit=bit, done=done):
            own = owner(z, c)
            if own is None or (a ^ own) & done or not (a ^ own) >> bit & 1:
                return None
            return (a ^ (1 << bit), z, c)

        terms.append(lay.send(total.astype(jnp.bfloat16), where))
        done |= 1 << bit
    return terms


def local(lay, integrals, coefficients, pair_rows, pair_cols, pair_count, row_blocks):
    aux_count, slots, block, _ = integrals.shape
    block_total = row_blocks.shape[0]
    own_blocks = block_total // lay.occ
    width = own_blocks * block
    orbitals = coefficients.shape[1]
    planes = lay.planes
    a = lax.axis_index("aux")
    occ_index = lax.axis_index("occ")
    z, c = occ_index // CORES, occ_index % CORES

    share = min(lay.aux, own_blocks)
    part = own_blocks // share
    blocks = coefficients.reshape(own_blocks, block, orbitals)
    mine = lax.dynamic_slice_in_dim(blocks, (a % share) * part, part, 0)
    other = lambda v: lay.send(v, lambda a_, z_, c_: (a_, z_, 1 - c_))
    pieces = [blocks, other(blocks)]
    meta = jnp.concatenate([v.reshape(1, -1) for v in (pair_count, pair_cols, pair_rows, row_blocks)], axis=1)
    for group in plane_groups(planes):
        far = [lay.send(mine, lambda a_, z_, c_, d=d: (a_, z_ ^ d, c_)) for d in group]
        far = jnp.concatenate(far, axis=0) if len(far) > 1 else far[0]
        if group[-1] == planes - 1:
            far = after(far, meta)
        for k in range(share):
            piece = lay.send(far, lambda a_, z_, c_, k=k: (a_ ^ k, z_, c_)) if k else far
            pieces += [piece, other(piece)]
    mirrored = lay.aux == planes == own_blocks == 4
    half = half_transform(lay, share, mirrored, own_blocks, integrals, pieces, meta)

    if mirrored:
        return mirrored_exchange(lay, *half)

    half = half[0].reshape(width, -1)

    out_blocks = block_total * block // lay.aux // width
    x_first, y_first = tuple(range(lay.bits)), tuple(reversed(range(lay.bits)))
    entries = []

    def arrived(held, plane_of):
        def owner(z_, c_):
            plane = plane_of(z_)
            return None if plane is None else (plane * CORES + c_) // out_blocks

        same = reduce_to_owner(lay, product(held, half), owner, x_first)
        cross = reduce_to_owner(lay, product(other(held), half), lambda z_, c_: owner(z_, 1 - c_), y_first)
        entries.append((plane_of, same, cross))

    arrived(half, lambda z_: z_)
    up = down = half
    for s in range(1, planes):
        up = lay.send(up, lambda a_, z_, c_: (a_, z_ + 1, c_) if z_ + 1 < planes else None)
        down = lay.send(down, lambda a_, z_, c_: (a_, z_ - 1, c_) if z_ > 0 else None)
        below = lambda z_, s=s: z_ - s if z_ >= s else None
        above = lambda z_, s=s: z_ + s if z_ + s < planes else None
        if 2 * s < planes:
            arrived(up, below)
            arrived(down, above)
        else:
            both = jnp.where(z >= s, up, down)
            arrived(both, lambda z_, below=below, above=above: below(z_) if above(z_) is None else above(z_))

    results = []
    for t in range(out_blocks):
        row = a * out_blocks + t
        index = jnp.int32(0)
        branches = []
        for plane_of, same, cross in entries:
            plane = jnp.int32(-1)
            for z_ in range(planes):
                if plane_of(z_) is not None:
                    plane = jnp.where(z == z_, plane_of(z_), plane)
            for terms, core in ((same, c), (cross, 1 - c)):
                index = jnp.where(plane * CORES + core == row, len(branches), index)
                branches.append(lambda terms=terms: functools.reduce(lambda x, y: x + y.astype(jnp.float32), terms))
        results.append(lax.switch(index, branches))
    return jnp.concatenate(results, axis=0) if out_blocks > 1 else results[0]


def solution(mesh):
    lay = Layout(mesh.shape["aux"], mesh.shape["occ"])
    return jax.shard_map(
        functools.partial(local, lay),
        mesh=mesh,
        in_specs=(
            P("aux", "occ", None, None),
            P("occ", None),
            P("aux", "occ"),
            P("aux", "occ"),
            P("aux", "occ"),
            P(),
        ),
        out_specs=P("aux", "occ"),
        check_vma=False,
    )
```

```python
import functools
import math

import jax
import jax.numpy as jnp
from jax import lax
from jax.experimental import pallas as pl
from jax.experimental.pallas import tpu as pltpu
from jax.sharding import PartitionSpec as P

AXES = ("aux", "occ")
CORES = 2
VMEM_LIMIT = 12 * 1024 * 1024
VMEM_MOST = 60 * 1024 * 1024
ANY = pl.BlockSpec(memory_space=pl.ANY)
IN_SMEM = pl.BlockSpec(memory_space=pltpu.SMEM)
IN_VMEM = pl.BlockSpec(memory_space=pltpu.VMEM)


class Layout:
    def __init__(self, aux, occ):
        self.aux, self.occ, self.planes = aux, occ, occ // CORES
        self.bits = int(math.log2(aux))

    def send(self, value, where):
        pairs = []
        for a in range(self.aux):
            for z in range(self.planes):
                for c in range(CORES):
                    to = where(a, z, c)
                    if to is not None:
                        pairs.append((a * self.occ + z * CORES + c, to[0] * self.occ + to[1] * CORES + to[2]))
        return lax.ppermute(value, AXES, pairs)


def half_kernel(lay, share, sources, mirrored, meta, ints, *refs):
    pieces, (*outs, coeff, total, found, listed) = refs[:sources], refs[sources:]
    own_blocks = total.shape[0]
    part = own_blocks // share
    start = 0
    for piece in pieces:
        coeff[pl.ds(start, piece.shape[0])] = piece[...]
        start += piece.shape[0]
    aux_count, slots, block, _ = ints.shape
    cols_at, rows_at, natural_at = 1, 1 + slots, 1 + 2 * slots
    total[...] = jnp.zeros_like(total)
    orbitals = coeff.shape[2]
    occ_index = lax.axis_index("occ")
    z, c = occ_index // CORES, occ_index % CORES
    a = lax.axis_index("aux")
    k = a % share

    for row in range(own_blocks):
        found[row] = 0

    def enter(slot, carry):
        row = meta[0, rows_at + slot]
        at = found[row]
        listed[row, at] = slot
        found[row] = at + 1
        return carry

    lax.fori_loop(0, meta[0, 0], enter, 0)

    def coeff_block(slot):
        source = meta[0, natural_at + meta[0, cols_at + slot]]
        owner, inner = source // own_blocks, source % own_blocks
        z_off, c_off = (owner // CORES) ^ z, (owner % CORES) ^ c
        k_off, in_part = (inner // part) ^ k, inner % part
        near = c_off * own_blocks + inner
        base = jnp.int32(0)
        start = CORES * own_blocks
        for group in plane_groups(lay.planes):
            inside = (z_off >= group[0]) & (z_off <= group[-1])
            at = start + ((k_off * CORES + c_off) * len(group) + z_off - group[0]) * part + in_part
            base = jnp.where(inside, at, base)
            start += share * CORES * len(group) * part
        return coeff[jnp.where(z_off == 0, near, base)]

    def ints_block(slot):
        return jnp.concatenate([ints[p, slot] for p in range(aux_count)], axis=0)

    for row in range(own_blocks):
        number = found[row]
        place = row ^ a if mirrored else row

        def add_two(step, carry, row=row, number=number, place=place):
            one = listed[row, 2 * step]
            paired = 2 * step + 1 < number
            two = jnp.where(paired, listed[row, jnp.where(paired, 2 * step + 1, 2 * step)], one)
            second = ints_block(two)
            left = jnp.concatenate([ints_block(one), jnp.where(paired, second, jnp.zeros_like(second))], axis=1)
            right = jnp.concatenate([coeff_block(one), coeff_block(two)], axis=0)
            total[place] += jnp.dot(left, right, preferred_element_type=jnp.float32)
            return carry

        lax.fori_loop(0, (number + 1) // 2, add_two, 0)
    for row in range(own_blocks):
        for p in range(aux_count):
            value = total[row, pl.ds(p * block, block), :].astype(jnp.bfloat16)
            columns = pl.ds(p * orbitals, orbitals)
            outs[0][row, :, columns] = value
            if mirrored:
                outs[1 + row][0, :, columns] = value


def plane_groups(planes):
    return [list(range(1, planes))]


def half_transform(lay, share, mirrored, own_blocks, integrals, pieces, meta):
    aux_count, slots, block, _ = integrals.shape
    orbitals = pieces[0].shape[2]
    blocks = sum(piece.shape[0] for piece in pieces)
    sizes = [own_blocks]
    if mirrored:
        sizes += [1] * own_blocks
    return pl.pallas_call(
        functools.partial(half_kernel, lay, share, len(pieces), mirrored),
        out_shape=[jax.ShapeDtypeStruct((size, block, aux_count * orbitals), jnp.bfloat16) for size in sizes],
        in_specs=[IN_SMEM] + [IN_VMEM] * (1 + len(pieces)),
        out_specs=[IN_VMEM] * len(sizes),
        scratch_shapes=[
            pltpu.VMEM((blocks, block, orbitals), jnp.bfloat16),
            pltpu.VMEM((own_blocks, aux_count * block, orbitals), jnp.float32),
            pltpu.SMEM((own_blocks,), jnp.int32),
            pltpu.SMEM((own_blocks, slots), jnp.int32),
        ],
        compiler_params=pltpu.CompilerParams(vmem_limit_bytes=VMEM_LIMIT),
        name="half_transform",
    )(meta, integrals, *pieces)


ROWS = (((1,), (1,)), ((), ()))


def dot_rows(first, second):
    return lax.dot_general(first, second, ROWS, preferred_element_type=jnp.float32)


def pair_kernel(*refs):
    *ins, near_ref, far_ref = refs
    rows, held = ins[:2], ins[2:]
    count, n, depth = held[0].shape
    for s in range(CORES):
        totals = [None] * count
        for k in range(count):
            quarter = jnp.concatenate([part[k] for part in rows], axis=0)
            value = dot_rows(held[s * count + k][...].reshape(count * n, depth), quarter)
            for m in range(count):
                part = value[(m ^ k) * n : ((m ^ k) + 1) * n]
                totals[m] = part if totals[m] is None else totals[m] + part
        for m in range(count):
            at = pl.ds((s * count + m) * n, n)
            near_ref[at, :] = totals[m][:, :n].astype(jnp.bfloat16)
            far_ref[at, :] = totals[m][:, n:].astype(jnp.bfloat16)


def pair_blocks(rows, held):
    count, n, _ = held[0].shape
    shape = jax.ShapeDtypeStruct((CORES * count * n, n), jnp.bfloat16)
    return pl.pallas_call(
        pair_kernel,
        out_shape=[shape] * len(rows),
        in_specs=[IN_VMEM] * (len(rows) + len(held)),
        out_specs=[IN_VMEM] * len(rows),
        compiler_params=pltpu.CompilerParams(vmem_limit_bytes=VMEM_LIMIT),
        name="pair_blocks",
    )(*rows, *held)


def own_kernel(*refs):
    *held, out_ref, plane, sems = refs
    _, count, rows, depth = plane.shape
    n = rows // count
    a = lax.axis_index("aux")
    occ_index = lax.axis_index("occ")
    z, c = occ_index // CORES, occ_index % CORES

    def moves(s, k):
        parts = [(held[s * count + k].at[m ^ k], plane.at[s, k, pl.ds(m * n, n)]) for m in range(count)]
        return [pltpu.make_async_copy(x, y, sems.at[s, k, m]) for m, (x, y) in enumerate(parts)]

    @pl.when(a == z)
    def _():
        copies = {(s, k): moves(s, k) for s in range(CORES) for k in range(count)}
        for parts in copies.values():
            for copy in parts:
                copy.start()
        for s in range(CORES):
            core = c if s == 0 else 1 - c
            total = None
            for k in range(count):
                for copy in copies[s, k]:
                    copy.wait()
                value = dot_rows(plane[s, k], plane[0, k])
                total = value if total is None else total + value
            for m in range(count):
                row = pl.multiple_of(core * rows + (a ^ m) * n, n)
                for col in range(count):
                    out_ref[pl.ds(row, n), pl.ds(pl.multiple_of((a ^ col) * n, n), n)] = total[
                        m * n : (m + 1) * n, col * n : (col + 1) * n
                    ]


def own_block(held):
    count, n, depth = held[0].shape
    return pl.pallas_call(
        own_kernel,
        out_shape=jax.ShapeDtypeStruct((CORES * count * n, count * n), jnp.float32),
        in_specs=[ANY] * len(held),
        out_specs=IN_VMEM,
        scratch_shapes=[
            pltpu.VMEM((CORES, count, count * n, depth), jnp.bfloat16),
            pltpu.SemaphoreType.DMA((CORES, count, count)),
        ],
        compiler_params=pltpu.CompilerParams(vmem_limit_bytes=VMEM_MOST),
        name="own_block",
    )(*held)


def place_kernel(*refs):
    *quarters, own_ref, out_ref = refs
    count = len(quarters)
    n = quarters[0].shape[1]
    width = count * n
    a = lax.axis_index("aux")
    occ_index = lax.axis_index("occ")
    z, c = occ_index // CORES, occ_index % CORES
    apart = lax.rem(a - z + count, count)

    def tile(row, col, value):
        out_ref[pl.ds(pl.multiple_of(row, n), n), pl.ds(pl.multiple_of(col, n), n)] = value

    @pl.when(apart == 0)
    def _():
        out_ref[...] = own_ref[...]

    @pl.when((apart > 0) & (apart <= count // 2))
    def _():
        for k, quarter in enumerate(quarters):
            for s in range(CORES):
                row = (c if s == 0 else 1 - c) * width + (a ^ k) * n
                for m in range(count):
                    value = quarter[pl.ds((s * count + m) * n, n), :].astype(jnp.float32)
                    tile(row, (a ^ k ^ m) * n, value.T)

    @pl.when(apart > count // 2)
    def _():
        for k, quarter in enumerate(quarters):
            for s in range(CORES):
                core = c if s == 0 else 1 - c
                for m in range(count):
                    value = quarter[pl.ds((s * count + m) * n, n), :].astype(jnp.float32)
                    tile(core * width + (a ^ k ^ m) * n, (a ^ k) * n, value)


def place_blocks(quarters, out):
    return pl.pallas_call(
        place_kernel,
        out_shape=jax.ShapeDtypeStruct(out.shape, out.dtype),
        in_specs=[IN_VMEM] * (len(quarters) + 1),
        out_specs=IN_VMEM,
        compiler_params=pltpu.CompilerParams(vmem_limit_bytes=VMEM_LIMIT),
        name="place_blocks",
    )(*quarters, out)


def after(value, *done):
    return lax.optimization_barrier((value, *done))[0]


def mirrored_exchange(lay, half, *sent):
    count, n, _ = half.shape
    a = lax.axis_index("aux")
    z = lax.axis_index("occ") // CORES
    other = lambda v: lay.send(v, lambda a_, z_, c_: (a_, z_, 1 - c_))
    toward = lambda v, k: lay.send(v, lambda a_, z_, c_: (a_ ^ k, z_, c_))
    below = lambda v, k=0: lay.send(v, lambda a_, z_, c_: (a_ ^ k, (z_ - 1) % count, c_))

    ahead = [below(sent[k], k) for k in range(count)]
    rows = [jnp.concatenate(ahead)]
    rows.append(below(rows[0]))
    first, second = (toward(half, k) for k in (1, 2))
    passed = jnp.concatenate([toward(first[: count // 2], 2), toward(second[count // 2 :], 1)])
    held = [half, first, second, passed]
    held += [other(v) for v in held[:-1]] + [other(after(passed, rows[1]))]

    blocks = pair_blocks(rows, held)
    mirror = lay.send(blocks[0], lambda a_, z_, c_: (a_, (z_ + 1) % count, c_))
    out = own_block(held)
    width = count * n
    blocks = [jnp.concatenate([v[:width], other(v[width:])]) for v in blocks]
    apart = {1: blocks[0], 2: after(blocks[1], out), 3: mirror}

    quarters = []
    for k in range(count):
        distance = lax.rem((a ^ k) - z + count, count)
        value = apart[1]
        for d in range(2, count):
            value = jnp.where(distance == d, apart[d], value)
        if k:
            value = lay.send(value, lambda a_, z_, c_: (a_ ^ k, z_, c_) if a_ ^ k != z_ else None)
        quarters.append(value)
    return place_blocks(quarters, out)


def product(first, second):
    return lax.dot_general(first, second, (((1,), (1,)), ((), ())), preferred_element_type=jnp.float32)


def reduce_to_owner(lay, partial, owner, order):
    terms = [partial]
    done = 0
    for step, bit in enumerate(order):
        total = functools.reduce(lambda x, y: x + y.astype(jnp.float32), terms)

        def where(a, z, c, bit=bit, done=done):
            own = owner(z, c)
            if own is None or (a ^ own) & done or not (a ^ own) >> bit & 1:
                return None
            return (a ^ (1 << bit), z, c)

        terms.append(lay.send(total.astype(jnp.bfloat16), where))
        done |= 1 << bit
    return terms


def local(lay, integrals, coefficients, pair_rows, pair_cols, pair_count, row_blocks):
    aux_count, slots, block, _ = integrals.shape
    block_total = row_blocks.shape[0]
    own_blocks = block_total // lay.occ
    width = own_blocks * block
    orbitals = coefficients.shape[1]
    planes = lay.planes
    a = lax.axis_index("aux")
    occ_index = lax.axis_index("occ")
    z, c = occ_index // CORES, occ_index % CORES

    share = min(lay.aux, own_blocks)
    part = own_blocks // share
    blocks = coefficients.reshape(own_blocks, block, orbitals)
    mine = lax.dynamic_slice_in_dim(blocks, (a % share) * part, part, 0)
    other = lambda v: lay.send(v, lambda a_, z_, c_: (a_, z_, 1 - c_))
    pieces = [blocks, other(blocks)]
    meta = jnp.concatenate([v.reshape(1, -1) for v in (pair_count, pair_cols, pair_rows, row_blocks)], axis=1)
    for group in plane_groups(planes):
        far = [lay.send(mine, lambda a_, z_, c_, d=d: (a_, z_ ^ d, c_)) for d in group]
        far = jnp.concatenate(far, axis=0) if len(far) > 1 else far[0]
        if group[-1] == planes - 1:
            far = after(far, meta)
        for k in range(share):
            piece = lay.send(far, lambda a_, z_, c_, k=k: (a_ ^ k, z_, c_)) if k else far
            pieces += [piece, other(piece)]
    mirrored = lay.aux == planes == own_blocks == 4
    half = half_transform(lay, share, mirrored, own_blocks, integrals, pieces, meta)

    if mirrored:
        return mirrored_exchange(lay, *half)

    half = half[0].reshape(width, -1)

    out_blocks = block_total * block // lay.aux // width
    x_first, y_first = tuple(range(lay.bits)), tuple(reversed(range(lay.bits)))
    entries = []

    def arrived(held, plane_of):
        def owner(z_, c_):
            plane = plane_of(z_)
            return None if plane is None else (plane * CORES + c_) // out_blocks

        same = reduce_to_owner(lay, product(held, half), owner, x_first)
        cross = reduce_to_owner(lay, product(other(held), half), lambda z_, c_: owner(z_, 1 - c_), y_first)
        entries.append((plane_of, same, cross))

    arrived(half, lambda z_: z_)
    up = down = half
    for s in range(1, planes):
        up = lay.send(up, lambda a_, z_, c_: (a_, z_ + 1, c_) if z_ + 1 < planes else None)
        down = lay.send(down, lambda a_, z_, c_: (a_, z_ - 1, c_) if z_ > 0 else None)
        below = lambda z_, s=s: z_ - s if z_ >= s else None
        above = lambda z_, s=s: z_ + s if z_ + s < planes else None
        if 2 * s < planes:
            arrived(up, below)
            arrived(down, above)
        else:
            both = jnp.where(z >= s, up, down)
            arrived(both, lambda z_, below=below, above=above: below(z_) if above(z_) is None else above(z_))

    results = []
    for t in range(out_blocks):
        row = a * out_blocks + t
        index = jnp.int32(0)
        branches = []
        for plane_of, same, cross in entries:
            plane = jnp.int32(-1)
            for z_ in range(planes):
                if plane_of(z_) is not None:
                    plane = jnp.where(z == z_, plane_of(z_), plane)
            for terms, core in ((same, c), (cross, 1 - c)):
                index = jnp.where(plane * CORES + core == row, len(branches), index)
                branches.append(lambda terms=terms: functools.reduce(lambda x, y: x + y.astype(jnp.float32), terms))
        results.append(lax.switch(index, branches))
    return jnp.concatenate(results, axis=0) if out_blocks > 1 else results[0]


def solution(mesh):
    lay = Layout(mesh.shape["aux"], mesh.shape["occ"])
    return jax.shard_map(
        functools.partial(local, lay),
        mesh=mesh,
        in_specs=(
            P("aux", "occ", None, None),
            P("occ", None),
            P("aux", "occ"),
            P("aux", "occ"),
            P("aux", "occ"),
            P(),
        ),
        out_specs=P("aux", "occ"),
        check_vma=False,
    )
```

```python
import functools
import math

import jax
import jax.numpy as jnp
from jax import lax
from jax.experimental import pallas as pl
from jax.experimental.pallas import tpu as pltpu
from jax.sharding import PartitionSpec as P

AXES = ("aux", "occ")
CORES = 2
TOGETHER = 4
VMEM_LIMIT = 12 * 1024 * 1024
VMEM_MOST = 60 * 1024 * 1024
ANY = pl.BlockSpec(memory_space=pl.ANY)
IN_SMEM = pl.BlockSpec(memory_space=pltpu.SMEM)
IN_VMEM = pl.BlockSpec(memory_space=pltpu.VMEM)


class Layout:
    def __init__(self, aux, occ):
        self.aux, self.occ, self.planes = aux, occ, occ // CORES
        self.bits = int(math.log2(aux))

    def send(self, value, where):
        pairs = []
        for a in range(self.aux):
            for z in range(self.planes):
                for c in range(CORES):
                    to = where(a, z, c)
                    if to is not None:
                        pairs.append((a * self.occ + z * CORES + c, to[0] * self.occ + to[1] * CORES + to[2]))
        return lax.ppermute(value, AXES, pairs)


def half_kernel(lay, share, sources, mirrored, meta, ints, *refs):
    pieces, (*outs, coeff, total, found, listed) = refs[:sources], refs[sources:]
    own_blocks = total.shape[0]
    part = own_blocks // share
    start = 0
    for piece in pieces:
        coeff[pl.ds(start, piece.shape[0])] = piece[...]
        start += piece.shape[0]
    aux_count, slots, block, _ = ints.shape
    cols_at, rows_at, natural_at = 1, 1 + slots, 1 + 2 * slots
    total[...] = jnp.zeros_like(total)
    orbitals = coeff.shape[2]
    occ_index = lax.axis_index("occ")
    z, c = occ_index // CORES, occ_index % CORES
    a = lax.axis_index("aux")
    k = a % share

    for row in range(own_blocks):
        found[row] = 0

    def enter(slot, carry):
        row = meta[0, rows_at + slot]
        at = found[row]
        listed[row, at] = slot
        found[row] = at + 1
        return carry

    lax.fori_loop(0, meta[0, 0], enter, 0)

    def coeff_block(slot):
        source = meta[0, natural_at + meta[0, cols_at + slot]]
        owner, inner = source // own_blocks, source % own_blocks
        z_off, c_off = (owner // CORES) ^ z, (owner % CORES) ^ c
        k_off, in_part = (inner // part) ^ k, inner % part
        near = c_off * own_blocks + inner
        base = jnp.int32(0)
        start = CORES * own_blocks
        for group in plane_groups(lay.planes):
            inside = (z_off >= group[0]) & (z_off <= group[-1])
            at = start + ((k_off * CORES + c_off) * len(group) + z_off - group[0]) * part + in_part
            base = jnp.where(inside, at, base)
            start += share * CORES * len(group) * part
        return coeff[jnp.where(z_off == 0, near, base)]

    def ints_block(slot):
        return jnp.concatenate([ints[p, slot] for p in range(aux_count)], axis=0)

    for row in range(own_blocks):
        number = found[row]
        place = row ^ a if mirrored else row

        def add_some(step, carry, row=row, number=number, place=place):
            lefts, rights = [], []
            for i in range(TOGETHER):
                at = TOGETHER * step + i
                there = at < number
                slot = listed[row, jnp.where(there, at, 0)]
                left = ints_block(slot)
                lefts.append(left if i == 0 else jnp.where(there, left, jnp.zeros_like(left)))
                rights.append(coeff_block(slot))
            left, right = jnp.concatenate(lefts, axis=1), jnp.concatenate(rights, axis=0)
            total[place] += jnp.dot(left, right, preferred_element_type=jnp.float32)
            return carry

        lax.fori_loop(0, (number + TOGETHER - 1) // TOGETHER, add_some, 0)
    for row in range(own_blocks):
        for p in range(aux_count):
            value = total[row, pl.ds(p * block, block), :].astype(jnp.bfloat16)
            columns = pl.ds(p * orbitals, orbitals)
            outs[0][row ^ a if mirrored else row, :, columns] = value
            if mirrored:
                outs[1 + row][0, :, columns] = value


def plane_groups(planes):
    return [list(range(1, planes))]


def half_transform(lay, share, mirrored, own_blocks, integrals, pieces, meta):
    aux_count, slots, block, _ = integrals.shape
    orbitals = pieces[0].shape[2]
    blocks = sum(piece.shape[0] for piece in pieces)
    sizes = [own_blocks]
    if mirrored:
        sizes += [1] * own_blocks
    return pl.pallas_call(
        functools.partial(half_kernel, lay, share, len(pieces), mirrored),
        out_shape=[jax.ShapeDtypeStruct((size, block, aux_count * orbitals), jnp.bfloat16) for size in sizes],
        in_specs=[IN_SMEM] + [IN_VMEM] * (1 + len(pieces)),
        out_specs=[IN_VMEM] * len(sizes),
        scratch_shapes=[
            pltpu.VMEM((blocks, block, orbitals), jnp.bfloat16),
            pltpu.VMEM((own_blocks, aux_count * block, orbitals), jnp.float32),
            pltpu.SMEM((own_blocks,), jnp.int32),
            pltpu.SMEM((own_blocks, slots), jnp.int32),
        ],
        compiler_params=pltpu.CompilerParams(vmem_limit_bytes=VMEM_LIMIT),
        name="half_transform",
    )(meta, integrals, *pieces)


ROWS = (((1,), (1,)), ((), ()))


def dot_rows(first, second):
    return lax.dot_general(first, second, ROWS, preferred_element_type=jnp.float32)


def places_held(core, s):
    beside = 1 + (core ^ s)
    return [0, beside, 3 - beside, 3]


def pair_kernel(*refs):
    one_ref, two_ref, *held, near_ref, far_ref = refs
    count, n, depth = one_ref.shape
    core = lax.axis_index("occ") % CORES
    for s in range(CORES):
        total = None
        for j, k in enumerate(places_held(core, s)):
            quarter = jnp.concatenate([one_ref[k], two_ref[k]], axis=0)
            value = dot_rows(held[s * count + j][...].reshape(count * n, depth), quarter)
            total = value if total is None else total + value
        rows = pl.ds(s * count * n, count * n)
        near_ref[rows, :] = total[:, :n].astype(jnp.bfloat16)
        far_ref[rows, :] = total[:, n:].astype(jnp.bfloat16)


def pair_blocks(rows, held):
    count, n, _ = held[0].shape
    shape = jax.ShapeDtypeStruct((CORES * count * n, n), jnp.bfloat16)
    return pl.pallas_call(
        pair_kernel,
        out_shape=[shape] * len(rows),
        in_specs=[IN_VMEM] * (len(rows) + len(held)),
        out_specs=[IN_VMEM] * len(rows),
        compiler_params=pltpu.CompilerParams(vmem_limit_bytes=VMEM_LIMIT),
        name="pair_blocks",
    )(*rows, *held)


def own_kernel(*refs):
    *held, out_ref, plane, sems = refs
    _, count, _, n, depth = plane.shape
    occ_index = lax.axis_index("occ")
    z, c = occ_index // CORES, occ_index % CORES

    @pl.when(lax.axis_index("aux") == z)
    def _():
        copies = [
            pltpu.make_async_copy(held[s * count + j], plane.at[s, j], sems.at[s, j])
            for s in range(CORES)
            for j in range(count)
        ]
        for copy in copies:
            copy.start()
        for s in range(CORES):
            total = None
            for j in range(count):
                copies[s * count + j].wait()
                own = plane[0, j if s == 0 else (0, 2, 1, 3)[j]].reshape(count * n, depth)
                value = dot_rows(plane[s, j].reshape(count * n, depth), own)
                total = value if total is None else total + value
            core = c if s == 0 else 1 - c
            out_ref[pl.ds(pl.multiple_of(core * count * n, n), count * n), :] = total


def own_block(held):
    count, n, depth = held[0].shape
    return pl.pallas_call(
        own_kernel,
        out_shape=jax.ShapeDtypeStruct((CORES * count * n, count * n), jnp.float32),
        in_specs=[ANY] * len(held),
        out_specs=IN_VMEM,
        scratch_shapes=[
            pltpu.VMEM((CORES, count, count, n, depth), jnp.bfloat16),
            pltpu.SemaphoreType.DMA((CORES, count)),
        ],
        compiler_params=pltpu.CompilerParams(vmem_limit_bytes=VMEM_MOST),
        name="own_block",
    )(*held)


def place_kernel(*refs):
    *quarters, own_ref, out_ref, laid, sems = refs
    count = len(quarters)
    n = quarters[0].shape[1]
    width = count * n
    a = lax.axis_index("aux")
    occ_index = lax.axis_index("occ")
    z, c = occ_index // CORES, occ_index % CORES
    apart = lax.rem(a - z + count, count)
    core = lambda s: c if s == 0 else 1 - c

    def tile(row, col, value):
        laid[pl.ds(pl.multiple_of(row, n), n), pl.ds(pl.multiple_of(col, n), n)] = value

    def leave(row, sem):
        rows = pl.ds(pl.multiple_of(row, n), n)
        copy = pltpu.make_async_copy(laid.at[rows], out_ref.at[rows], sem)
        copy.start()
        return copy

    @pl.when(apart == 0)
    def _():
        copy = pltpu.make_async_copy(own_ref, out_ref, sems.at[0])
        copy.start()
        copy.wait()

    @pl.when((apart > 0) & (apart <= count // 2))
    def _():
        copies = []
        for k, quarter in enumerate(quarters):
            for s in range(CORES):
                row = core(s) * width + (a ^ k) * n
                for m in range(count):
                    value = quarter[pl.ds((s * count + m) * n, n), :].astype(jnp.float32)
                    tile(row, m * n, value.T)
                copies.append(leave(row, sems.at[len(copies)]))
        for copy in copies:
            copy.wait()

    @pl.when(apart > count // 2)
    def _():
        copies = []
        for s in range(CORES):
            for m in range(count):
                row = core(s) * width + m * n
                for k, quarter in enumerate(quarters):
                    value = quarter[pl.ds((s * count + m) * n, n), :].astype(jnp.float32)
                    tile(row, (a ^ k) * n, value)
                copies.append(leave(row, sems.at[len(copies)]))
        for copy in copies:
            copy.wait()


def place_blocks(quarters, out):
    return pl.pallas_call(
        place_kernel,
        out_shape=jax.ShapeDtypeStruct(out.shape, out.dtype),
        in_specs=[IN_VMEM] * (len(quarters) + 1),
        out_specs=ANY,
        scratch_shapes=[pltpu.VMEM(out.shape, out.dtype), pltpu.SemaphoreType.DMA((CORES * len(quarters),))],
        compiler_params=pltpu.CompilerParams(vmem_limit_bytes=VMEM_LIMIT),
        name="place_blocks",
    )(*quarters, out)


def after(value, *done):
    return lax.optimization_barrier((value, *done))[0]


def mirrored_exchange(lay, half, *sent):
    count, n, _ = half.shape
    a = lax.axis_index("aux")
    z = lax.axis_index("occ") // CORES
    other = lambda v: lay.send(v, lambda a_, z_, c_: (a_, z_, 1 - c_))
    toward = lambda v, k: lay.send(v, lambda a_, z_, c_: (a_ ^ k, z_, c_))
    below = lambda v, k=0: lay.send(v, lambda a_, z_, c_: (a_ ^ k, (z_ - 1) % count, c_))

    ahead = [below(sent[k], k) for k in range(count)]
    rows = [jnp.concatenate(ahead)]
    rows.append(below(rows[0]))
    one_way = lambda v: lay.send(v, lambda a_, z_, c_: (a_ ^ (1 + c_), z_, c_))
    other_way = lambda v: lay.send(v, lambda a_, z_, c_: (a_ ^ (2 - c_), z_, c_))
    beside = one_way(half)
    held = [half, beside, other_way(half), other_way(beside)]
    held += [other(v) for v in held[:-1]] + [other(after(held[-1], rows[1]))]

    blocks = pair_blocks(rows, held)
    mirror = lay.send(blocks[0], lambda a_, z_, c_: (a_, (z_ + 1) % count, c_))
    out = own_block(held)
    width = count * n
    blocks = [jnp.concatenate([v[:width], other(v[width:])]) for v in blocks]
    apart = {1: blocks[0], 2: after(blocks[1], out), 3: mirror}

    quarters = []
    for k in range(count):
        distance = lax.rem((a ^ k) - z + count, count)
        value = apart[1]
        for d in range(2, count):
            value = jnp.where(distance == d, apart[d], value)
        if k:
            value = lay.send(value, lambda a_, z_, c_: (a_ ^ k, z_, c_) if a_ ^ k != z_ else None)
        quarters.append(value)
    return place_blocks(quarters, out)


def product(first, second):
    return lax.dot_general(first, second, (((1,), (1,)), ((), ())), preferred_element_type=jnp.float32)


def reduce_to_owner(lay, partial, owner, order):
    terms = [partial]
    done = 0
    for step, bit in enumerate(order):
        total = functools.reduce(lambda x, y: x + y.astype(jnp.float32), terms)

        def where(a, z, c, bit=bit, done=done):
            own = owner(z, c)
            if own is None or (a ^ own) & done or not (a ^ own) >> bit & 1:
                return None
            return (a ^ (1 << bit), z, c)

        terms.append(lay.send(total.astype(jnp.bfloat16), where))
        done |= 1 << bit
    return terms


def local(lay, integrals, coefficients, pair_rows, pair_cols, pair_count, row_blocks):
    aux_count, slots, block, _ = integrals.shape
    block_total = row_blocks.shape[0]
    own_blocks = block_total // lay.occ
    width = own_blocks * block
    orbitals = coefficients.shape[1]
    planes = lay.planes
    a = lax.axis_index("aux")
    occ_index = lax.axis_index("occ")
    z, c = occ_index // CORES, occ_index % CORES

    share = min(lay.aux, own_blocks)
    part = own_blocks // share
    blocks = coefficients.reshape(own_blocks, block, orbitals)
    mine = lax.dynamic_slice_in_dim(blocks, (a % share) * part, part, 0)
    other = lambda v: lay.send(v, lambda a_, z_, c_: (a_, z_, 1 - c_))
    traded = other(blocks)
    pieces = [other(traded), traded]
    meta = jnp.concatenate([v.reshape(1, -1) for v in (pair_count, pair_cols, pair_rows, row_blocks)], axis=1)
    for group in plane_groups(planes):
        far = [lay.send(mine, lambda a_, z_, c_, d=d: (a_, z_ ^ d, c_)) for d in group]
        far = jnp.concatenate(far, axis=0) if len(far) > 1 else far[0]
        if group[-1] == planes - 1:
            far = after(far, meta)
        for k in range(share):
            piece = lay.send(far, lambda a_, z_, c_, k=k: (a_ ^ k, z_, c_)) if k else far
            pieces += [piece, other(piece)]
    mirrored = lay.aux == planes == own_blocks == 4
    half = half_transform(lay, share, mirrored, own_blocks, integrals, pieces, meta)

    if mirrored:
        return mirrored_exchange(lay, *half)

    half = half[0].reshape(width, -1)

    out_blocks = block_total * block // lay.aux // width
    x_first, y_first = tuple(range(lay.bits)), tuple(reversed(range(lay.bits)))
    entries = []

    def arrived(held, plane_of):
        def owner(z_, c_):
            plane = plane_of(z_)
            return None if plane is None else (plane * CORES + c_) // out_blocks

        same = reduce_to_owner(lay, product(held, half), owner, x_first)
        cross = reduce_to_owner(lay, product(other(held), half), lambda z_, c_: owner(z_, 1 - c_), y_first)
        entries.append((plane_of, same, cross))

    arrived(half, lambda z_: z_)
    up = down = half
    for s in range(1, planes):
        up = lay.send(up, lambda a_, z_, c_: (a_, z_ + 1, c_) if z_ + 1 < planes else None)
        down = lay.send(down, lambda a_, z_, c_: (a_, z_ - 1, c_) if z_ > 0 else None)
        below = lambda z_, s=s: z_ - s if z_ >= s else None
        above = lambda z_, s=s: z_ + s if z_ + s < planes else None
        if 2 * s < planes:
            arrived(up, below)
            arrived(down, above)
        else:
            both = jnp.where(z >= s, up, down)
            arrived(both, lambda z_, below=below, above=above: below(z_) if above(z_) is None else above(z_))

    results = []
    for t in range(out_blocks):
        row = a * out_blocks + t
        index = jnp.int32(0)
        branches = []
        for plane_of, same, cross in entries:
            plane = jnp.int32(-1)
            for z_ in range(planes):
                if plane_of(z_) is not None:
                    plane = jnp.where(z == z_, plane_of(z_), plane)
            for terms, core in ((same, c), (cross, 1 - c)):
                index = jnp.where(plane * CORES + core == row, len(branches), index)
                branches.append(lambda terms=terms: functools.reduce(lambda x, y: x + y.astype(jnp.float32), terms))
        results.append(lax.switch(index, branches))
    return jnp.concatenate(results, axis=0) if out_blocks > 1 else results[0]


def solution(mesh):
    lay = Layout(mesh.shape["aux"], mesh.shape["occ"])
    return jax.shard_map(
        functools.partial(local, lay),
        mesh=mesh,
        in_specs=(
            P("aux", "occ", None, None),
            P("occ", None),
            P("aux", "occ"),
            P("aux", "occ"),
            P("aux", "occ"),
            P(),
        ),
        out_specs=P("aux", "occ"),
        check_vma=False,
    )
```

```python
import functools
import math

import jax
import jax.numpy as jnp
from jax import lax
from jax.experimental import pallas as pl
from jax.experimental.pallas import tpu as pltpu
from jax.sharding import PartitionSpec as P

AXES = ("aux", "occ")
CORES = 2
TOGETHER = 4
VMEM_LIMIT = 30 * 1024 * 1024
VMEM_MOST = 60 * 1024 * 1024
ANY = pl.BlockSpec(memory_space=pl.ANY)
IN_SMEM = pl.BlockSpec(memory_space=pltpu.SMEM)
IN_VMEM = pl.BlockSpec(memory_space=pltpu.VMEM)


class Layout:
    def __init__(self, aux, occ):
        self.aux, self.occ, self.planes = aux, occ, occ // CORES
        self.bits = int(math.log2(aux))

    def send(self, value, where):
        pairs = []
        for a in range(self.aux):
            for z in range(self.planes):
                for c in range(CORES):
                    to = where(a, z, c)
                    if to is not None:
                        pairs.append((a * self.occ + z * CORES + c, to[0] * self.occ + to[1] * CORES + to[2]))
        return lax.ppermute(value, AXES, pairs)


def half_kernel(lay, share, sources, mirrored, meta, ints, *refs):
    pieces, (*outs, coeff, total, found, listed) = refs[:sources], refs[sources:]
    own_blocks = total.shape[0]
    part = own_blocks // share
    start = 0
    for piece in pieces:
        coeff[pl.ds(start, piece.shape[0])] = piece[...]
        start += piece.shape[0]
    aux_count, slots, block, _ = ints.shape
    cols_at, rows_at, natural_at = 1, 1 + slots, 1 + 2 * slots
    total[...] = jnp.zeros_like(total)
    orbitals = coeff.shape[2]
    occ_index = lax.axis_index("occ")
    z, c = occ_index // CORES, occ_index % CORES
    a = lax.axis_index("aux")
    k = a % share

    for row in range(own_blocks):
        found[row] = 0

    def enter(slot, carry):
        row = meta[0, rows_at + slot]
        at = found[row]
        listed[row, at] = slot
        found[row] = at + 1
        return carry

    lax.fori_loop(0, meta[0, 0], enter, 0)

    def coeff_block(slot):
        source = meta[0, natural_at + meta[0, cols_at + slot]]
        owner, inner = source // own_blocks, source % own_blocks
        z_off, c_off = (owner // CORES) ^ z, (owner % CORES) ^ c
        k_off, in_part = (inner // part) ^ k, inner % part
        near = c_off * own_blocks + inner
        base = jnp.int32(0)
        start = CORES * own_blocks
        for group in plane_groups(lay.planes):
            inside = (z_off >= group[0]) & (z_off <= group[-1])
            at = start + ((k_off * CORES + c_off) * len(group) + z_off - group[0]) * part + in_part
            base = jnp.where(inside, at, base)
            start += share * CORES * len(group) * part
        return coeff[jnp.where(z_off == 0, near, base)]

    def ints_block(slot):
        return jnp.concatenate([ints[p, slot] for p in range(aux_count)], axis=0)

    for row in range(own_blocks):
        number = found[row]
        place = row ^ a if mirrored else row

        def add_some(step, carry, row=row, number=number, place=place):
            lefts, rights = [], []
            for i in range(TOGETHER):
                at = TOGETHER * step + i
                there = at < number
                slot = listed[row, jnp.where(there, at, 0)]
                left = ints_block(slot)
                lefts.append(left if i == 0 else jnp.where(there, left, jnp.zeros_like(left)))
                rights.append(coeff_block(slot))
            left, right = jnp.concatenate(lefts, axis=1), jnp.concatenate(rights, axis=0)
            total[place] += jnp.dot(left, right, preferred_element_type=jnp.float32)
            return carry

        lax.fori_loop(0, (number + TOGETHER - 1) // TOGETHER, add_some, 0)
    for row in range(own_blocks):
        for p in range(aux_count):
            value = total[row, pl.ds(p * block, block), :].astype(jnp.bfloat16)
            columns = pl.ds(p * orbitals, orbitals)
            outs[0][row ^ a if mirrored else row, :, columns] = value
            if mirrored:
                outs[1 + row][0, :, columns] = value


def plane_groups(planes):
    return [list(range(1, planes))]


def half_transform(lay, share, mirrored, own_blocks, integrals, pieces, meta):
    aux_count, slots, block, _ = integrals.shape
    orbitals = pieces[0].shape[2]
    blocks = sum(piece.shape[0] for piece in pieces)
    sizes = [own_blocks]
    if mirrored:
        sizes += [1] * own_blocks
    return pl.pallas_call(
        functools.partial(half_kernel, lay, share, len(pieces), mirrored),
        out_shape=[jax.ShapeDtypeStruct((size, block, aux_count * orbitals), jnp.bfloat16) for size in sizes],
        in_specs=[IN_SMEM] + [IN_VMEM] * (1 + len(pieces)),
        out_specs=[IN_VMEM] * len(sizes),
        scratch_shapes=[
            pltpu.VMEM((blocks, block, orbitals), jnp.bfloat16),
            pltpu.VMEM((own_blocks, aux_count * block, orbitals), jnp.float32),
            pltpu.SMEM((own_blocks,), jnp.int32),
            pltpu.SMEM((own_blocks, slots), jnp.int32),
        ],
        compiler_params=pltpu.CompilerParams(vmem_limit_bytes=VMEM_LIMIT),
        name="half_transform",
    )(meta, integrals, *pieces)


ROWS = (((1,), (1,)), ((), ()))


def dot_rows(first, second):
    return lax.dot_general(first, second, ROWS, preferred_element_type=jnp.float32)


def places_held(core, s):
    beside = 1 + (core ^ s)
    return [0, beside, 3 - beside, 3]


def pair_kernel(*refs):
    one_ref, two_ref, *held, near_ref, far_ref = refs
    count, n, depth = one_ref.shape
    core = lax.axis_index("occ") % CORES
    for s in range(CORES):
        total = None
        for j, k in enumerate(places_held(core, s)):
            quarter = jnp.concatenate([one_ref[k], two_ref[k]], axis=0)
            value = dot_rows(held[s * count + j][...].reshape(count * n, depth), quarter)
            total = value if total is None else total + value
        rows = pl.ds(s * count * n, count * n)
        near_ref[rows, :] = total[:, :n].astype(jnp.bfloat16)
        far_ref[rows, :] = total[:, n:].astype(jnp.bfloat16)


def pair_blocks(rows, held):
    count, n, _ = held[0].shape
    shape = jax.ShapeDtypeStruct((CORES * count * n, n), jnp.bfloat16)
    return pl.pallas_call(
        pair_kernel,
        out_shape=[shape] * len(rows),
        in_specs=[IN_VMEM] * (len(rows) + len(held)),
        out_specs=[IN_VMEM] * len(rows),
        compiler_params=pltpu.CompilerParams(vmem_limit_bytes=VMEM_LIMIT),
        name="pair_blocks",
    )(*rows, *held)


def own_kernel(*refs):
    *held, out_ref, plane, sems = refs
    _, count, _, n, depth = plane.shape
    occ_index = lax.axis_index("occ")
    z, c = occ_index // CORES, occ_index % CORES

    @pl.when(lax.axis_index("aux") == z)
    def _():
        copies = [
            pltpu.make_async_copy(held[s * count + j], plane.at[s, j], sems.at[s, j])
            for s in range(CORES)
            for j in range(count)
        ]
        for copy in copies:
            copy.start()
        for s in range(CORES):
            total = None
            for j in range(count):
                copies[s * count + j].wait()
                own = plane[0, j if s == 0 else (0, 2, 1, 3)[j]].reshape(count * n, depth)
                value = dot_rows(plane[s, j].reshape(count * n, depth), own)
                total = value if total is None else total + value
            core = c if s == 0 else 1 - c
            out_ref[pl.ds(pl.multiple_of(core * count * n, n), count * n), :] = total


def own_block(held):
    count, n, depth = held[0].shape
    return pl.pallas_call(
        own_kernel,
        out_shape=jax.ShapeDtypeStruct((CORES * count * n, count * n), jnp.float32),
        in_specs=[ANY] * len(held),
        out_specs=IN_VMEM,
        scratch_shapes=[
            pltpu.VMEM((CORES, count, count, n, depth), jnp.bfloat16),
            pltpu.SemaphoreType.DMA((CORES, count)),
        ],
        compiler_params=pltpu.CompilerParams(vmem_limit_bytes=VMEM_MOST),
        name="own_block",
    )(*held)


def place_kernel(*refs):
    *quarters, own_ref, out_ref, laid, sems = refs
    count = len(quarters)
    n = quarters[0].shape[1]
    width = count * n
    a = lax.axis_index("aux")
    occ_index = lax.axis_index("occ")
    z, c = occ_index // CORES, occ_index % CORES
    apart = lax.rem(a - z + count, count)
    core = lambda s: c if s == 0 else 1 - c

    def tile(row, col, value):
        laid[pl.ds(pl.multiple_of(row, n), n), pl.ds(pl.multiple_of(col, n), n)] = value

    def leave(row, sem):
        rows = pl.ds(pl.multiple_of(row, n), n)
        copy = pltpu.make_async_copy(laid.at[rows], out_ref.at[rows], sem)
        copy.start()
        return copy

    @pl.when(apart == 0)
    def _():
        copy = pltpu.make_async_copy(own_ref, out_ref, sems.at[0])
        copy.start()
        copy.wait()

    @pl.when((apart > 0) & (apart <= count // 2))
    def _():
        copies = []
        for k, quarter in enumerate(quarters):
            for s in range(CORES):
                row = core(s) * width + (a ^ k) * n
                for m in range(count):
                    value = quarter[pl.ds((s * count + m) * n, n), :].astype(jnp.float32)
                    tile(row, m * n, value.T)
                copies.append(leave(row, sems.at[len(copies)]))
        for copy in copies:
            copy.wait()

    @pl.when(apart > count // 2)
    def _():
        copies = []
        for s in range(CORES):
            for m in range(count):
                row = core(s) * width + m * n
                for k, quarter in enumerate(quarters):
                    value = quarter[pl.ds((s * count + m) * n, n), :].astype(jnp.float32)
                    tile(row, (a ^ k) * n, value)
                copies.append(leave(row, sems.at[len(copies)]))
        for copy in copies:
            copy.wait()


def place_blocks(quarters, out):
    return pl.pallas_call(
        place_kernel,
        out_shape=jax.ShapeDtypeStruct(out.shape, out.dtype),
        in_specs=[IN_VMEM] * (len(quarters) + 1),
        out_specs=ANY,
        scratch_shapes=[pltpu.VMEM(out.shape, out.dtype), pltpu.SemaphoreType.DMA((CORES * len(quarters),))],
        compiler_params=pltpu.CompilerParams(vmem_limit_bytes=VMEM_LIMIT),
        name="place_blocks",
    )(*quarters, out)


def after(value, *done):
    return lax.optimization_barrier((value, *done))[0]


def mirrored_exchange(lay, half, *sent):
    count, n, _ = half.shape
    a = lax.axis_index("aux")
    z = lax.axis_index("occ") // CORES
    other = lambda v: lay.send(v, lambda a_, z_, c_: (a_, z_, 1 - c_))
    toward = lambda v, k: lay.send(v, lambda a_, z_, c_: (a_ ^ k, z_, c_))
    below = lambda v, k=0: lay.send(v, lambda a_, z_, c_: (a_ ^ k, (z_ - 1) % count, c_))

    ahead = [below(sent[k], k) for k in range(count)]
    rows = [jnp.concatenate(ahead)]
    rows.append(below(rows[0]))
    one_way = lambda v: lay.send(v, lambda a_, z_, c_: (a_ ^ (1 + c_), z_, c_))
    other_way = lambda v: lay.send(v, lambda a_, z_, c_: (a_ ^ (2 - c_), z_, c_))
    beside = one_way(half)
    held = [half, beside, other_way(half), other_way(beside)]
    held += [other(v) for v in held[:-1]] + [other(after(held[-1], rows[1]))]

    blocks = pair_blocks(rows, held)
    mirror = lay.send(blocks[0], lambda a_, z_, c_: (a_, (z_ + 1) % count, c_))
    out = own_block(held)
    width = count * n
    blocks = [jnp.concatenate([v[:width], other(v[width:])]) for v in blocks]
    apart = {1: after(blocks[0], out), 2: blocks[1], 3: mirror}

    quarters = []
    for k in range(count):
        distance = lax.rem((a ^ k) - z + count, count)
        value = apart[1]
        for d in range(2, count):
            value = jnp.where(distance == d, apart[d], value)
        if k:
            value = lay.send(value, lambda a_, z_, c_: (a_ ^ k, z_, c_) if a_ ^ k != z_ else None)
        quarters.append(value)
    return place_blocks(quarters, out)


def product(first, second):
    return lax.dot_general(first, second, (((1,), (1,)), ((), ())), preferred_element_type=jnp.float32)


def reduce_to_owner(lay, partial, owner, order):
    terms = [partial]
    done = 0
    for step, bit in enumerate(order):
        total = functools.reduce(lambda x, y: x + y.astype(jnp.float32), terms)

        def where(a, z, c, bit=bit, done=done):
            own = owner(z, c)
            if own is None or (a ^ own) & done or not (a ^ own) >> bit & 1:
                return None
            return (a ^ (1 << bit), z, c)

        terms.append(lay.send(total.astype(jnp.bfloat16), where))
        done |= 1 << bit
    return terms


def local(lay, integrals, coefficients, pair_rows, pair_cols, pair_count, row_blocks):
    aux_count, slots, block, _ = integrals.shape
    block_total = row_blocks.shape[0]
    own_blocks = block_total // lay.occ
    width = own_blocks * block
    orbitals = coefficients.shape[1]
    planes = lay.planes
    a = lax.axis_index("aux")
    occ_index = lax.axis_index("occ")
    z, c = occ_index // CORES, occ_index % CORES

    share = min(lay.aux, own_blocks)
    part = own_blocks // share
    blocks = coefficients.reshape(own_blocks, block, orbitals)
    mine = lax.dynamic_slice_in_dim(blocks, (a % share) * part, part, 0)
    other = lambda v: lay.send(v, lambda a_, z_, c_: (a_, z_, 1 - c_))
    traded = other(blocks)
    pieces = [other(traded), traded]
    meta = jnp.concatenate([v.reshape(1, -1) for v in (pair_count, pair_cols, pair_rows, row_blocks)], axis=1)
    for group in plane_groups(planes):
        far = [lay.send(mine, lambda a_, z_, c_, d=d: (a_, z_ ^ d, c_)) for d in group]
        far = jnp.concatenate(far, axis=0) if len(far) > 1 else far[0]
        if group[-1] == planes - 1:
            far = after(far, meta)
        for k in range(share):
            piece = lay.send(far, lambda a_, z_, c_, k=k: (a_ ^ k, z_, c_)) if k else far
            pieces += [piece, other(piece)]
    mirrored = lay.aux == planes == own_blocks == 4
    half = half_transform(lay, share, mirrored, own_blocks, integrals, pieces, meta)

    if mirrored:
        return mirrored_exchange(lay, *half)

    half = half[0].reshape(width, -1)

    out_blocks = block_total * block // lay.aux // width
    x_first, y_first = tuple(range(lay.bits)), tuple(reversed(range(lay.bits)))
    entries = []

    def arrived(held, plane_of):
        def owner(z_, c_):
            plane = plane_of(z_)
            return None if plane is None else (plane * CORES + c_) // out_blocks

        same = reduce_to_owner(lay, product(held, half), owner, x_first)
        cross = reduce_to_owner(lay, product(other(held), half), lambda z_, c_: owner(z_, 1 - c_), y_first)
        entries.append((plane_of, same, cross))

    arrived(half, lambda z_: z_)
    up = down = half
    for s in range(1, planes):
        up = lay.send(up, lambda a_, z_, c_: (a_, z_ + 1, c_) if z_ + 1 < planes else None)
        down = lay.send(down, lambda a_, z_, c_: (a_, z_ - 1, c_) if z_ > 0 else None)
        below = lambda z_, s=s: z_ - s if z_ >= s else None
        above = lambda z_, s=s: z_ + s if z_ + s < planes else None
        if 2 * s < planes:
            arrived(up, below)
            arrived(down, above)
        else:
            both = jnp.where(z >= s, up, down)
            arrived(both, lambda z_, below=below, above=above: below(z_) if above(z_) is None else above(z_))

    results = []
    for t in range(out_blocks):
        row = a * out_blocks + t
        index = jnp.int32(0)
        branches = []
        for plane_of, same, cross in entries:
            plane = jnp.int32(-1)
            for z_ in range(planes):
                if plane_of(z_) is not None:
                    plane = jnp.where(z == z_, plane_of(z_), plane)
            for terms, core in ((same, c), (cross, 1 - c)):
                index = jnp.where(plane * CORES + core == row, len(branches), index)
                branches.append(lambda terms=terms: functools.reduce(lambda x, y: x + y.astype(jnp.float32), terms))
        results.append(lax.switch(index, branches))
    return jnp.concatenate(results, axis=0) if out_blocks > 1 else results[0]


def solution(mesh):
    lay = Layout(mesh.shape["aux"], mesh.shape["occ"])
    return jax.shard_map(
        functools.partial(local, lay),
        mesh=mesh,
        in_specs=(
            P("aux", "occ", None, None),
            P("occ", None),
            P("aux", "occ"),
            P("aux", "occ"),
            P("aux", "occ"),
            P(),
        ),
        out_specs=P("aux", "occ"),
        check_vma=False,
    )
```

```python
import functools
import math

import jax
import jax.numpy as jnp
from jax import lax
from jax.experimental import pallas as pl
from jax.experimental.pallas import tpu as pltpu
from jax.sharding import PartitionSpec as P

AXES = ("aux", "occ")
CORES = 2
TOGETHER = 4
VMEM_LIMIT = 30 * 1024 * 1024
VMEM_MOST = 60 * 1024 * 1024
ANY = pl.BlockSpec(memory_space=pl.ANY)
IN_SMEM = pl.BlockSpec(memory_space=pltpu.SMEM)
IN_VMEM = pl.BlockSpec(memory_space=pltpu.VMEM)


class Layout:
    def __init__(self, aux, occ):
        self.aux, self.occ, self.planes = aux, occ, occ // CORES
        self.bits = int(math.log2(aux))

    def send(self, value, where):
        pairs = []
        for a in range(self.aux):
            for z in range(self.planes):
                for c in range(CORES):
                    to = where(a, z, c)
                    if to is not None:
                        pairs.append((a * self.occ + z * CORES + c, to[0] * self.occ + to[1] * CORES + to[2]))
        return lax.ppermute(value, AXES, pairs)


def half_kernel(lay, share, sources, mirrored, meta, ints, *refs):
    pieces, (*outs, coeff, total, found, listed) = refs[:sources], refs[sources:]
    own_blocks = total.shape[0]
    part = own_blocks // share
    start = 0
    for piece in pieces:
        coeff[pl.ds(start, piece.shape[0])] = piece[...]
        start += piece.shape[0]
    aux_count, slots, block, _ = ints.shape
    cols_at, rows_at, natural_at = 1, 1 + slots, 1 + 2 * slots
    total[...] = jnp.zeros_like(total)
    orbitals = coeff.shape[2]
    occ_index = lax.axis_index("occ")
    z, c = occ_index // CORES, occ_index % CORES
    a = lax.axis_index("aux")
    k = a % share

    for row in range(own_blocks):
        found[row] = 0

    def enter(slot, carry):
        row = meta[0, rows_at + slot]
        at = found[row]
        listed[row, at] = slot
        found[row] = at + 1
        return carry

    lax.fori_loop(0, meta[0, 0], enter, 0)

    def coeff_block(slot):
        source = meta[0, natural_at + meta[0, cols_at + slot]]
        owner, inner = source // own_blocks, source % own_blocks
        z_off, c_off = (owner // CORES) ^ z, (owner % CORES) ^ c
        k_off, in_part = (inner // part) ^ k, inner % part
        near = c_off * own_blocks + inner
        base = jnp.int32(0)
        start = CORES * own_blocks
        for group in plane_groups(lay.planes):
            inside = (z_off >= group[0]) & (z_off <= group[-1])
            at = start + ((k_off * CORES + c_off) * len(group) + z_off - group[0]) * part + in_part
            base = jnp.where(inside, at, base)
            start += share * CORES * len(group) * part
        return coeff[jnp.where(z_off == 0, near, base)]

    def ints_block(slot):
        return jnp.concatenate([ints[p, slot] for p in range(aux_count)], axis=0)

    for row in range(own_blocks):
        number = found[row]
        place = row ^ a if mirrored else row

        def add_some(step, carry, row=row, number=number, place=place):
            lefts, rights = [], []
            for i in range(TOGETHER):
                at = TOGETHER * step + i
                there = at < number
                slot = listed[row, jnp.where(there, at, 0)]
                left = ints_block(slot)
                lefts.append(left if i == 0 else jnp.where(there, left, jnp.zeros_like(left)))
                rights.append(coeff_block(slot))
            left, right = jnp.concatenate(lefts, axis=1), jnp.concatenate(rights, axis=0)
            total[place] += jnp.dot(left, right, preferred_element_type=jnp.float32)
            return carry

        lax.fori_loop(0, (number + TOGETHER - 1) // TOGETHER, add_some, 0)
    for row in range(own_blocks):
        for p in range(aux_count):
            value = total[row, pl.ds(p * block, block), :].astype(jnp.bfloat16)
            columns = pl.ds(p * orbitals, orbitals)
            outs[0][row ^ a if mirrored else row, :, columns] = value
            if mirrored:
                outs[1 + row][0, :, columns] = value


def plane_groups(planes):
    return [list(range(1, planes))]


def half_transform(lay, share, mirrored, own_blocks, integrals, pieces, meta):
    aux_count, slots, block, _ = integrals.shape
    orbitals = pieces[0].shape[2]
    blocks = sum(piece.shape[0] for piece in pieces)
    sizes = [own_blocks]
    if mirrored:
        sizes += [1] * own_blocks
    return pl.pallas_call(
        functools.partial(half_kernel, lay, share, len(pieces), mirrored),
        out_shape=[jax.ShapeDtypeStruct((size, block, aux_count * orbitals), jnp.bfloat16) for size in sizes],
        in_specs=[IN_SMEM] + [IN_VMEM] * (1 + len(pieces)),
        out_specs=[IN_VMEM] * len(sizes),
        scratch_shapes=[
            pltpu.VMEM((blocks, block, orbitals), jnp.bfloat16),
            pltpu.VMEM((own_blocks, aux_count * block, orbitals), jnp.float32),
            pltpu.SMEM((own_blocks,), jnp.int32),
            pltpu.SMEM((own_blocks, slots), jnp.int32),
        ],
        compiler_params=pltpu.CompilerParams(vmem_limit_bytes=VMEM_LIMIT),
        name="half_transform",
    )(meta, integrals, *pieces)


ROWS = (((1,), (1,)), ((), ()))


def dot_rows(first, second):
    return lax.dot_general(first, second, ROWS, preferred_element_type=jnp.float32)


def places_held(core, s):
    beside = 1 + (core ^ s)
    return [0, beside, 3 - beside, 3]


def pair_kernel(*refs):
    one_ref, two_ref, *held, near_ref, far_ref = refs
    count, n, depth = one_ref.shape
    core = lax.axis_index("occ") % CORES
    for s in range(CORES):
        total = None
        for j, k in enumerate(places_held(core, s)):
            quarter = jnp.concatenate([one_ref[k], two_ref[k]], axis=0)
            value = dot_rows(held[s * count + j][...].reshape(count * n, depth), quarter)
            total = value if total is None else total + value
        rows = pl.ds(s * count * n, count * n)
        near_ref[rows, :] = total[:, :n].astype(jnp.bfloat16)
        far_ref[rows, :] = total[:, n:].astype(jnp.bfloat16)


def pair_blocks(rows, held):
    count, n, _ = held[0].shape
    shape = jax.ShapeDtypeStruct((CORES * count * n, n), jnp.bfloat16)
    return pl.pallas_call(
        pair_kernel,
        out_shape=[shape] * len(rows),
        in_specs=[IN_VMEM] * (len(rows) + len(held)),
        out_specs=[IN_VMEM] * len(rows),
        compiler_params=pltpu.CompilerParams(vmem_limit_bytes=VMEM_LIMIT),
        name="pair_blocks",
    )(*rows, *held)


def own_kernel(*refs):
    *held, out_ref, plane, sems = refs
    _, count, _, n, depth = plane.shape
    occ_index = lax.axis_index("occ")
    z, c = occ_index // CORES, occ_index % CORES

    @pl.when(lax.axis_index("aux") == z)
    def _():
        copies = [
            pltpu.make_async_copy(held[s * count + j], plane.at[s, j], sems.at[s, j])
            for s in range(CORES)
            for j in range(count)
        ]
        for copy in copies:
            copy.start()
        for s in range(CORES):
            total = None
            for j in range(count):
                copies[s * count + j].wait()
                own = plane[0, j if s == 0 else (0, 2, 1, 3)[j]].reshape(count * n, depth)
                value = dot_rows(plane[s, j].reshape(count * n, depth), own)
                total = value if total is None else total + value
            core = c if s == 0 else 1 - c
            out_ref[pl.ds(pl.multiple_of(core * count * n, n), count * n), :] = total


def own_block(held):
    count, n, depth = held[0].shape
    return pl.pallas_call(
        own_kernel,
        out_shape=jax.ShapeDtypeStruct((CORES * count * n, count * n), jnp.float32),
        in_specs=[ANY] * len(held),
        out_specs=IN_VMEM,
        scratch_shapes=[
            pltpu.VMEM((CORES, count, count, n, depth), jnp.bfloat16),
            pltpu.SemaphoreType.DMA((CORES, count)),
        ],
        compiler_params=pltpu.CompilerParams(vmem_limit_bytes=VMEM_MOST),
        name="own_block",
    )(*held)


def place_kernel(*refs):
    *quarters, own_ref, out_ref, laid, sems = refs
    count = len(quarters)
    n = quarters[0].shape[1]
    width = count * n
    a = lax.axis_index("aux")
    occ_index = lax.axis_index("occ")
    z, c = occ_index // CORES, occ_index % CORES
    apart = lax.rem(a - z + count, count)
    core = lambda s: c if s == 0 else 1 - c

    def tile(row, col, value):
        laid[pl.ds(pl.multiple_of(row, n), n), pl.ds(pl.multiple_of(col, n), n)] = value

    def leave(row, sem):
        rows = pl.ds(pl.multiple_of(row, n), n)
        copy = pltpu.make_async_copy(laid.at[rows], out_ref.at[rows], sem)
        copy.start()
        return copy

    @pl.when(apart == 0)
    def _():
        copy = pltpu.make_async_copy(own_ref, out_ref, sems.at[0])
        copy.start()
        copy.wait()

    @pl.when((apart > 0) & (apart <= count // 2))
    def _():
        copies = []
        for k, quarter in zip(places_held(c, 0), quarters):
            for s in range(CORES):
                row = core(s) * width + (a ^ k) * n
                for m in range(count):
                    value = quarter[pl.ds((s * count + m) * n, n), :].astype(jnp.float32)
                    tile(row, m * n, value.T)
                copies.append(leave(row, sems.at[len(copies)]))
        for copy in copies:
            copy.wait()

    @pl.when(apart > count // 2)
    def _():
        copies = []
        for s in range(CORES):
            for m in range(count):
                row = core(s) * width + m * n
                for k, quarter in zip(places_held(c, 0), quarters):
                    value = quarter[pl.ds((s * count + m) * n, n), :].astype(jnp.float32)
                    tile(row, (a ^ k) * n, value)
                copies.append(leave(row, sems.at[len(copies)]))
        for copy in copies:
            copy.wait()


def place_blocks(quarters, out):
    return pl.pallas_call(
        place_kernel,
        out_shape=jax.ShapeDtypeStruct(out.shape, out.dtype),
        in_specs=[IN_VMEM] * (len(quarters) + 1),
        out_specs=ANY,
        scratch_shapes=[pltpu.VMEM(out.shape, out.dtype), pltpu.SemaphoreType.DMA((CORES * len(quarters),))],
        compiler_params=pltpu.CompilerParams(vmem_limit_bytes=VMEM_LIMIT),
        name="place_blocks",
    )(*quarters, out)


def after(value, *done):
    return lax.optimization_barrier((value, *done))[0]


def mirrored_exchange(lay, half, *sent):
    count, n, _ = half.shape
    a = lax.axis_index("aux")
    z = lax.axis_index("occ") // CORES
    other = lambda v: lay.send(v, lambda a_, z_, c_: (a_, z_, 1 - c_))
    toward = lambda v, k: lay.send(v, lambda a_, z_, c_: (a_ ^ k, z_, c_))
    below = lambda v, k=0: lay.send(v, lambda a_, z_, c_: (a_ ^ k, (z_ - 1) % count, c_))

    ahead = [below(sent[k], k) for k in range(count)]
    rows = [jnp.concatenate(ahead)]
    rows.append(below(rows[0]))
    one_way = lambda v: lay.send(v, lambda a_, z_, c_: (a_ ^ (1 + c_), z_, c_))
    other_way = lambda v: lay.send(v, lambda a_, z_, c_: (a_ ^ (2 - c_), z_, c_))
    beside = one_way(half)
    held = [half, beside, other_way(half), other_way(beside)]
    held += [other(v) for v in held[:-1]] + [other(after(held[-1], rows[1]))]

    blocks = pair_blocks(rows, held)
    mirror = lay.send(blocks[0], lambda a_, z_, c_: (a_, (z_ + 1) % count, c_))
    out = own_block(held)
    width = count * n
    blocks = [jnp.concatenate([v[:width], other(v[width:])]) for v in blocks]
    apart = {1: after(blocks[0], out), 2: blocks[1], 3: mirror}

    core = lax.axis_index("occ") % CORES
    quarters = []
    for j in range(count):
        distance = lax.rem((a ^ places_held(core, 0)[j]) - z + count, count)
        value = apart[1]
        for d in range(2, count):
            value = jnp.where(distance == d, apart[d], value)
        if j:

            def where(a_, z_, c_, j=j):
                place = a_ ^ places_held(c_, 0)[j]
                return (place, z_, c_) if place != z_ else None

            value = lay.send(value, where)
        quarters.append(value)
    return place_blocks(quarters, out)


def product(first, second):
    return lax.dot_general(first, second, (((1,), (1,)), ((), ())), preferred_element_type=jnp.float32)


def reduce_to_owner(lay, partial, owner, order):
    terms = [partial]
    done = 0
    for step, bit in enumerate(order):
        total = functools.reduce(lambda x, y: x + y.astype(jnp.float32), terms)

        def where(a, z, c, bit=bit, done=done):
            own = owner(z, c)
            if own is None or (a ^ own) & done or not (a ^ own) >> bit & 1:
                return None
            return (a ^ (1 << bit), z, c)

        terms.append(lay.send(total.astype(jnp.bfloat16), where))
        done |= 1 << bit
    return terms


def local(lay, integrals, coefficients, pair_rows, pair_cols, pair_count, row_blocks):
    aux_count, slots, block, _ = integrals.shape
    block_total = row_blocks.shape[0]
    own_blocks = block_total // lay.occ
    width = own_blocks * block
    orbitals = coefficients.shape[1]
    planes = lay.planes
    a = lax.axis_index("aux")
    occ_index = lax.axis_index("occ")
    z, c = occ_index // CORES, occ_index % CORES

    share = min(lay.aux, own_blocks)
    part = own_blocks // share
    blocks = coefficients.reshape(own_blocks, block, orbitals)
    mine = lax.dynamic_slice_in_dim(blocks, (a % share) * part, part, 0)
    other = lambda v: lay.send(v, lambda a_, z_, c_: (a_, z_, 1 - c_))
    traded = other(blocks)
    pieces = [other(traded), traded]
    meta = jnp.concatenate([v.reshape(1, -1) for v in (pair_count, pair_cols, pair_rows, row_blocks)], axis=1)
    for group in plane_groups(planes):
        far = [lay.send(mine, lambda a_, z_, c_, d=d: (a_, z_ ^ d, c_)) for d in group]
        far = jnp.concatenate(far, axis=0) if len(far) > 1 else far[0]
        if group[-1] == planes - 1:
            far = after(far, meta)
        for k in range(share):
            piece = lay.send(far, lambda a_, z_, c_, k=k: (a_ ^ k, z_, c_)) if k else far
            pieces += [piece, other(piece)]
    mirrored = lay.aux == planes == own_blocks == 4
    half = half_transform(lay, share, mirrored, own_blocks, integrals, pieces, meta)

    if mirrored:
        return mirrored_exchange(lay, *half)

    half = half[0].reshape(width, -1)

    out_blocks = block_total * block // lay.aux // width
    x_first, y_first = tuple(range(lay.bits)), tuple(reversed(range(lay.bits)))
    entries = []

    def arrived(held, plane_of):
        def owner(z_, c_):
            plane = plane_of(z_)
            return None if plane is None else (plane * CORES + c_) // out_blocks

        same = reduce_to_owner(lay, product(held, half), owner, x_first)
        cross = reduce_to_owner(lay, product(other(held), half), lambda z_, c_: owner(z_, 1 - c_), y_first)
        entries.append((plane_of, same, cross))

    arrived(half, lambda z_: z_)
    up = down = half
    for s in range(1, planes):
        up = lay.send(up, lambda a_, z_, c_: (a_, z_ + 1, c_) if z_ + 1 < planes else None)
        down = lay.send(down, lambda a_, z_, c_: (a_, z_ - 1, c_) if z_ > 0 else None)
        below = lambda z_, s=s: z_ - s if z_ >= s else None
        above = lambda z_, s=s: z_ + s if z_ + s < planes else None
        if 2 * s < planes:
            arrived(up, below)
            arrived(down, above)
        else:
            both = jnp.where(z >= s, up, down)
            arrived(both, lambda z_, below=below, above=above: below(z_) if above(z_) is None else above(z_))

    results = []
    for t in range(out_blocks):
        row = a * out_blocks + t
        index = jnp.int32(0)
        branches = []
        for plane_of, same, cross in entries:
            plane = jnp.int32(-1)
            for z_ in range(planes):
                if plane_of(z_) is not None:
                    plane = jnp.where(z == z_, plane_of(z_), plane)
            for terms, core in ((same, c), (cross, 1 - c)):
                index = jnp.where(plane * CORES + core == row, len(branches), index)
                branches.append(lambda terms=terms: functools.reduce(lambda x, y: x + y.astype(jnp.float32), terms))
        results.append(lax.switch(index, branches))
    return jnp.concatenate(results, axis=0) if out_blocks > 1 else results[0]


def solution(mesh):
    lay = Layout(mesh.shape["aux"], mesh.shape["occ"])
    return jax.shard_map(
        functools.partial(local, lay),
        mesh=mesh,
        in_specs=(
            P("aux", "occ", None, None),
            P("occ", None),
            P("aux", "occ"),
            P("aux", "occ"),
            P("aux", "occ"),
            P(),
        ),
        out_specs=P("aux", "occ"),
        check_vma=False,
    )
```

```python
import functools
import math

import jax
import jax.numpy as jnp
from jax import lax
from jax.experimental import pallas as pl
from jax.experimental.pallas import tpu as pltpu
from jax.sharding import PartitionSpec as P

AXES = ("aux", "occ")
CORES = 2
TOGETHER = 4
VMEM_LIMIT = 30 * 1024 * 1024
VMEM_MOST = 60 * 1024 * 1024
ANY = pl.BlockSpec(memory_space=pl.ANY)
IN_SMEM = pl.BlockSpec(memory_space=pltpu.SMEM)
IN_VMEM = pl.BlockSpec(memory_space=pltpu.VMEM)


class Layout:
    def __init__(self, aux, occ):
        self.aux, self.occ, self.planes = aux, occ, occ // CORES
        self.bits = int(math.log2(aux))

    def send(self, value, where):
        pairs = []
        for a in range(self.aux):
            for z in range(self.planes):
                for c in range(CORES):
                    to = where(a, z, c)
                    if to is not None:
                        pairs.append((a * self.occ + z * CORES + c, to[0] * self.occ + to[1] * CORES + to[2]))
        return lax.ppermute(value, AXES, pairs)


def half_kernel(lay, share, sources, mirrored, meta, ints, *refs):
    pieces, (*outs, coeff, total, found, listed) = refs[:sources], refs[sources:]
    own_blocks = total.shape[0]
    part = own_blocks // share
    start = 0
    for piece in pieces:
        coeff[pl.ds(start, piece.shape[0])] = piece[...]
        start += piece.shape[0]
    aux_count, slots, block, _ = ints.shape
    cols_at, rows_at, natural_at = 1, 1 + slots, 1 + 2 * slots
    total[...] = jnp.zeros_like(total)
    orbitals = coeff.shape[2]
    occ_index = lax.axis_index("occ")
    z, c = occ_index // CORES, occ_index % CORES
    a = lax.axis_index("aux")
    k = a % share

    for row in range(own_blocks):
        found[row] = 0

    def enter(slot, carry):
        row = meta[0, rows_at + slot]
        at = found[row]
        listed[row, at] = slot
        found[row] = at + 1
        return carry

    lax.fori_loop(0, meta[0, 0], enter, 0)

    def coeff_block(slot):
        source = meta[0, natural_at + meta[0, cols_at + slot]]
        owner, inner = source // own_blocks, source % own_blocks
        z_off, c_off = (owner // CORES) ^ z, (owner % CORES) ^ c
        k_off, in_part = (inner // part) ^ k, inner % part
        near = c_off * own_blocks + inner
        base = jnp.int32(0)
        start = CORES * own_blocks
        for group in plane_groups(lay.planes):
            inside = (z_off >= group[0]) & (z_off <= group[-1])
            at = start + ((k_off * CORES + c_off) * len(group) + z_off - group[0]) * part + in_part
            base = jnp.where(inside, at, base)
            start += share * CORES * len(group) * part
        return coeff[jnp.where(z_off == 0, near, base)]

    def ints_block(slot):
        return jnp.concatenate([ints[p, slot] for p in range(aux_count)], axis=0)

    for row in range(own_blocks):
        number = found[row]
        place = row ^ a if mirrored else row

        def add_some(step, carry, row=row, number=number, place=place):
            lefts, rights = [], []
            for i in range(TOGETHER):
                at = TOGETHER * step + i
                there = at < number
                slot = listed[row, jnp.where(there, at, 0)]
                left = ints_block(slot)
                lefts.append(left if i == 0 else jnp.where(there, left, jnp.zeros_like(left)))
                rights.append(coeff_block(slot))
            left, right = jnp.concatenate(lefts, axis=1), jnp.concatenate(rights, axis=0)
            total[place] += jnp.dot(left, right, preferred_element_type=jnp.float32)
            return carry

        lax.fori_loop(0, (number + TOGETHER - 1) // TOGETHER, add_some, 0)
    for row in range(own_blocks):
        for p in range(aux_count):
            value = total[row, pl.ds(p * block, block), :].astype(jnp.bfloat16)
            columns = pl.ds(p * orbitals, orbitals)
            outs[0][row ^ a if mirrored else row, :, columns] = value
            if mirrored:
                outs[1 + row][0, :, columns] = value


def plane_groups(planes):
    return [list(range(1, planes))]


def half_transform(lay, share, mirrored, own_blocks, integrals, pieces, meta):
    aux_count, slots, block, _ = integrals.shape
    orbitals = pieces[0].shape[2]
    blocks = sum(piece.shape[0] for piece in pieces)
    sizes = [own_blocks]
    if mirrored:
        sizes += [1] * own_blocks
    return pl.pallas_call(
        functools.partial(half_kernel, lay, share, len(pieces), mirrored),
        out_shape=[jax.ShapeDtypeStruct((size, block, aux_count * orbitals), jnp.bfloat16) for size in sizes],
        in_specs=[IN_SMEM] + [IN_VMEM] * (1 + len(pieces)),
        out_specs=[IN_VMEM] * len(sizes),
        scratch_shapes=[
            pltpu.VMEM((blocks, block, orbitals), jnp.bfloat16),
            pltpu.VMEM((own_blocks, aux_count * block, orbitals), jnp.float32),
            pltpu.SMEM((own_blocks,), jnp.int32),
            pltpu.SMEM((own_blocks, slots), jnp.int32),
        ],
        compiler_params=pltpu.CompilerParams(vmem_limit_bytes=VMEM_LIMIT),
        name="half_transform",
    )(meta, integrals, *pieces)


ROWS = (((1,), (1,)), ((), ()))


def dot_rows(first, second):
    return lax.dot_general(first, second, ROWS, preferred_element_type=jnp.float32)


def places_held(core, s):
    beside = 1 + (core ^ s)
    return [0, beside, 3 - beside, 3]


def pair_kernel(*refs):
    one_ref, two_ref, *held, near_ref, far_ref = refs
    count, n, depth = one_ref.shape
    core = lax.axis_index("occ") % CORES
    for s in range(CORES):
        total = None
        for j, k in enumerate(places_held(core, s)):
            quarter = jnp.concatenate([one_ref[k], two_ref[k]], axis=0)
            value = dot_rows(held[s * count + j][...].reshape(count * n, depth), quarter)
            total = value if total is None else total + value
        rows = pl.ds(s * count * n, count * n)
        near_ref[rows, :] = total[:, :n].astype(jnp.bfloat16)
        far_ref[rows, :] = total[:, n:].astype(jnp.bfloat16)


def pair_blocks(rows, held):
    count, n, _ = held[0].shape
    shape = jax.ShapeDtypeStruct((CORES * count * n, n), jnp.bfloat16)
    return pl.pallas_call(
        pair_kernel,
        out_shape=[shape] * len(rows),
        in_specs=[IN_VMEM] * (len(rows) + len(held)),
        out_specs=[IN_VMEM] * len(rows),
        compiler_params=pltpu.CompilerParams(vmem_limit_bytes=VMEM_LIMIT),
        name="pair_blocks",
    )(*rows, *held)


def own_kernel(*refs):
    *held, out_ref, plane, sems = refs
    _, count, _, n, depth = plane.shape
    occ_index = lax.axis_index("occ")
    z, c = occ_index // CORES, occ_index % CORES

    @pl.when(lax.axis_index("aux") == z)
    def _():
        copies = [
            pltpu.make_async_copy(held[s * count + j], plane.at[s, j], sems.at[s, j])
            for s in range(CORES)
            for j in range(count)
        ]
        for copy in copies:
            copy.start()
        for s in range(CORES):
            total = None
            for j in range(count):
                copies[s * count + j].wait()
                own = plane[0, j if s == 0 else (0, 2, 1, 3)[j]].reshape(count * n, depth)
                value = dot_rows(plane[s, j].reshape(count * n, depth), own)
                total = value if total is None else total + value
            core = c if s == 0 else 1 - c
            out_ref[pl.ds(pl.multiple_of(core * count * n, n), count * n), :] = total


def own_block(held):
    count, n, depth = held[0].shape
    return pl.pallas_call(
        own_kernel,
        out_shape=jax.ShapeDtypeStruct((CORES * count * n, count * n), jnp.float32),
        in_specs=[ANY] * len(held),
        out_specs=IN_VMEM,
        scratch_shapes=[
            pltpu.VMEM((CORES, count, count, n, depth), jnp.bfloat16),
            pltpu.SemaphoreType.DMA((CORES, count)),
        ],
        compiler_params=pltpu.CompilerParams(vmem_limit_bytes=VMEM_MOST),
        name="own_block",
    )(*held)


def place_kernel(*refs):
    *quarters, own_ref, out_ref, laid, sems = refs
    count = len(quarters)
    n = quarters[0].shape[1]
    width = count * n
    a = lax.axis_index("aux")
    occ_index = lax.axis_index("occ")
    z, c = occ_index // CORES, occ_index % CORES
    apart = lax.rem(a - z + count, count)
    core = lambda s: c if s == 0 else 1 - c

    def tile(row, col, value):
        laid[pl.ds(pl.multiple_of(row, n), n), pl.ds(pl.multiple_of(col, n), n)] = value

    def leave(row, sem):
        rows = pl.ds(pl.multiple_of(row, n), n)
        copy = pltpu.make_async_copy(laid.at[rows], out_ref.at[rows], sem)
        copy.start()
        return copy

    @pl.when(apart == 0)
    def _():
        copy = pltpu.make_async_copy(own_ref, out_ref, sems.at[0])
        copy.start()
        copy.wait()

    @pl.when((apart > 0) & (apart <= count // 2))
    def _():
        copies = []
        for k, quarter in zip(places_held(c, 0), quarters):
            for s in range(CORES):
                row = core(s) * width + (a ^ k) * n
                for m in range(count):
                    value = quarter[pl.ds((s * count + m) * n, n), :].astype(jnp.float32)
                    tile(row, m * n, value.T)
                copies.append(leave(row, sems.at[len(copies)]))
        for copy in copies:
            copy.wait()

    @pl.when(apart > count // 2)
    def _():
        copies = []
        for s in range(CORES):
            for m in range(count):
                row = core(s) * width + m * n
                for k, quarter in zip(places_held(c, 0), quarters):
                    value = quarter[pl.ds((s * count + m) * n, n), :].astype(jnp.float32)
                    tile(row, (a ^ k) * n, value)
                copies.append(leave(row, sems.at[len(copies)]))
        for copy in copies:
            copy.wait()


def place_blocks(quarters, out):
    return pl.pallas_call(
        place_kernel,
        out_shape=jax.ShapeDtypeStruct(out.shape, out.dtype),
        in_specs=[IN_VMEM] * len(quarters) + [ANY],
        out_specs=ANY,
        scratch_shapes=[pltpu.VMEM(out.shape, out.dtype), pltpu.SemaphoreType.DMA((CORES * len(quarters),))],
        compiler_params=pltpu.CompilerParams(vmem_limit_bytes=VMEM_LIMIT),
        name="place_blocks",
    )(*quarters, out)


def after(value, *done):
    return lax.optimization_barrier((value, *done))[0]


def mirrored_exchange(lay, half, *sent):
    count, n, _ = half.shape
    a = lax.axis_index("aux")
    z = lax.axis_index("occ") // CORES
    other = lambda v: lay.send(v, lambda a_, z_, c_: (a_, z_, 1 - c_))
    toward = lambda v, k: lay.send(v, lambda a_, z_, c_: (a_ ^ k, z_, c_))
    below = lambda v, k=0: lay.send(v, lambda a_, z_, c_: (a_ ^ k, (z_ - 1) % count, c_))

    ahead = [below(sent[k], k) for k in range(count)]
    rows = [jnp.concatenate(ahead)]
    rows.append(below(rows[0]))
    one_way = lambda v: lay.send(v, lambda a_, z_, c_: (a_ ^ (1 + c_), z_, c_))
    other_way = lambda v: lay.send(v, lambda a_, z_, c_: (a_ ^ (2 - c_), z_, c_))
    beside = one_way(half)
    held = [half, beside, other_way(half), other_way(beside)]
    held += [other(v) for v in held[:-1]] + [other(after(held[-1], rows[1]))]

    blocks = pair_blocks(rows, held)
    mirror = lay.send(blocks[0], lambda a_, z_, c_: (a_, (z_ + 1) % count, c_))
    out = own_block(held)
    width = count * n
    blocks = [jnp.concatenate([v[:width], other(v[width:])]) for v in blocks]
    apart = {1: after(blocks[0], out), 2: blocks[1], 3: mirror}

    core = lax.axis_index("occ") % CORES
    quarters = []
    for j in range(count):
        distance = lax.rem((a ^ places_held(core, 0)[j]) - z + count, count)
        value = apart[1]
        for d in range(2, count):
            value = jnp.where(distance == d, apart[d], value)
        if j:

            def where(a_, z_, c_, j=j):
                place = a_ ^ places_held(c_, 0)[j]
                return (place, z_, c_) if place != z_ else None

            value = lay.send(value, where)
        quarters.append(value)
    return place_blocks(quarters, out)


def product(first, second):
    return lax.dot_general(first, second, (((1,), (1,)), ((), ())), preferred_element_type=jnp.float32)


def reduce_to_owner(lay, partial, owner, order):
    terms = [partial]
    done = 0
    for step, bit in enumerate(order):
        total = functools.reduce(lambda x, y: x + y.astype(jnp.float32), terms)

        def where(a, z, c, bit=bit, done=done):
            own = owner(z, c)
            if own is None or (a ^ own) & done or not (a ^ own) >> bit & 1:
                return None
            return (a ^ (1 << bit), z, c)

        terms.append(lay.send(total.astype(jnp.bfloat16), where))
        done |= 1 << bit
    return terms


def local(lay, integrals, coefficients, pair_rows, pair_cols, pair_count, row_blocks):
    aux_count, slots, block, _ = integrals.shape
    block_total = row_blocks.shape[0]
    own_blocks = block_total // lay.occ
    width = own_blocks * block
    orbitals = coefficients.shape[1]
    planes = lay.planes
    a = lax.axis_index("aux")
    occ_index = lax.axis_index("occ")
    z, c = occ_index // CORES, occ_index % CORES

    share = min(lay.aux, own_blocks)
    part = own_blocks // share
    blocks = coefficients.reshape(own_blocks, block, orbitals)
    mine = lax.dynamic_slice_in_dim(blocks, (a % share) * part, part, 0)
    other = lambda v: lay.send(v, lambda a_, z_, c_: (a_, z_, 1 - c_))
    traded = other(blocks)
    pieces = [other(traded), traded]
    meta = jnp.concatenate([v.reshape(1, -1) for v in (pair_count, pair_cols, pair_rows, row_blocks)], axis=1)
    for group in plane_groups(planes):
        far = [lay.send(mine, lambda a_, z_, c_, d=d: (a_, z_ ^ d, c_)) for d in group]
        far = jnp.concatenate(far, axis=0) if len(far) > 1 else far[0]
        if group[-1] == planes - 1:
            far = after(far, meta)
        for k in range(share):
            piece = lay.send(far, lambda a_, z_, c_, k=k: (a_ ^ k, z_, c_)) if k else far
            pieces += [piece, other(piece)]
    mirrored = lay.aux == planes == own_blocks == 4
    half = half_transform(lay, share, mirrored, own_blocks, integrals, pieces, meta)

    if mirrored:
        return mirrored_exchange(lay, *half)

    half = half[0].reshape(width, -1)

    out_blocks = block_total * block // lay.aux // width
    x_first, y_first = tuple(range(lay.bits)), tuple(reversed(range(lay.bits)))
    entries = []

    def arrived(held, plane_of):
        def owner(z_, c_):
            plane = plane_of(z_)
            return None if plane is None else (plane * CORES + c_) // out_blocks

        same = reduce_to_owner(lay, product(held, half), owner, x_first)
        cross = reduce_to_owner(lay, product(other(held), half), lambda z_, c_: owner(z_, 1 - c_), y_first)
        entries.append((plane_of, same, cross))

    arrived(half, lambda z_: z_)
    up = down = half
    for s in range(1, planes):
        up = lay.send(up, lambda a_, z_, c_: (a_, z_ + 1, c_) if z_ + 1 < planes else None)
        down = lay.send(down, lambda a_, z_, c_: (a_, z_ - 1, c_) if z_ > 0 else None)
        below = lambda z_, s=s: z_ - s if z_ >= s else None
        above = lambda z_, s=s: z_ + s if z_ + s < planes else None
        if 2 * s < planes:
            arrived(up, below)
            arrived(down, above)
        else:
            both = jnp.where(z >= s, up, down)
            arrived(both, lambda z_, below=below, above=above: below(z_) if above(z_) is None else above(z_))

    results = []
    for t in range(out_blocks):
        row = a * out_blocks + t
        index = jnp.int32(0)
        branches = []
        for plane_of, same, cross in entries:
            plane = jnp.int32(-1)
            for z_ in range(planes):
                if plane_of(z_) is not None:
                    plane = jnp.where(z == z_, plane_of(z_), plane)
            for terms, core in ((same, c), (cross, 1 - c)):
                index = jnp.where(plane * CORES + core == row, len(branches), index)
                branches.append(lambda terms=terms: functools.reduce(lambda x, y: x + y.astype(jnp.float32), terms))
        results.append(lax.switch(index, branches))
    return jnp.concatenate(results, axis=0) if out_blocks > 1 else results[0]


def solution(mesh):
    lay = Layout(mesh.shape["aux"], mesh.shape["occ"])
    return jax.shard_map(
        functools.partial(local, lay),
        mesh=mesh,
        in_specs=(
            P("aux", "occ", None, None),
            P("occ", None),
            P("aux", "occ"),
            P("aux", "occ"),
            P("aux", "occ"),
            P(),
        ),
        out_specs=P("aux", "occ"),
        check_vma=False,
    )
```
